32 devices in a mesh: mic: 8 (over y, x, core), tile: 4 (over z).
Axes of the slice: x: 2, y: 2, z: 4, core: 2. Of those that a mesh axis runs over, the one named last changes fastest.
Arguments:
- micrograph: bfloat16 [8, 447, 1536], P('mic', None, 'tile'), may hold values from -6 to 6
- templates: bfloat16 [8, 384, 384], P('mic'), may hold values from -6 to 6
- orient_ids: int32 [8], P('mic'), may hold values from 0 to 359
- defocus_bins: int32 [8], P('mic'), may hold values from 0 to 15
Outputs:
- peak_value: float32 [8, 64, 1536], P('mic', None, 'tile')
- corr_sum: float32 [8, 64, 1536], P('mic', None, 'tile')
- corr_sumsq: float32 [8, 64, 1536], P('mic', None, 'tile')
- orient_cos: float32 [8, 64, 1536], P('mic', None, 'tile')
- orient_sin: float32 [8, 64, 1536], P('mic', None, 'tile')
The draws below stay inside these ranges and needn't reach their ends.
All inputs are finite; a program needn't handle non-finite values.
Results may differ from the reference program's by a relative error of at most 0.013.
Values may be sent and summed in bfloat16 or wider, within the bound.
No kernel may reach another device: no remote copies, remote signals or barrier semaphores. Data moves between devices by JAX's collectives and lax.ppermute only.
A program may use at most 64 MiB of HBM per device.

```python
import math
import jax
import jax.numpy as jnp
from jax import lax

TS = 384
TC = 384
MH = 64
STEPS = 4
NANG = 360
NBINS = 16
MICS = 8
NCOL = 1536
MR = 447
MC = 767
LR = 448
LC = 768
HALF = 384
N_TILE = 4


def place_ends(result, key, low, high):
    longest = result.shape.index(max(result.shape))
    spots = []
    for shift in (0, 1):
        where = [jax.random.randint(jax.random.fold_in(key, axis), (), 0, length) for axis, length in enumerate(result.shape)]
        where[longest] = (where[longest] + shift) % result.shape[longest]
        spots.append(tuple(where))
    return result.at[spots[0]].set(low).at[spots[1]].set(high)


def block_levels(stream_key, shape, cuts, least, high):
    level = 1.0
    for dim, blocks in cuts:
        heights = jax.random.uniform(jax.random.fold_in(jax.random.fold_in(stream_key, 6), dim), (blocks,), jnp.float32, least / len(cuts), high / len(cuts))
        level = level * jnp.repeat(jnp.exp(heights), shape[dim] // blocks).reshape((-1,) + (1,) * (len(shape) - 1 - dim))
    return level


def noise(own_key, dims, scale, reach, cuts=(), kind=jnp.bfloat16):
    entries = jax.random.normal(own_key, dims, jnp.float32) * scale
    if len(cuts) > 0:
        entries = block_levels(own_key, dims, cuts, -0.22, 0.18) * entries
    return jnp.clip(entries, min=-reach, max=reach).astype(kind)


def setup_inputs(seed: int = 0) -> dict:
    splits = jax.random.split(jax.random.key(seed), 5)
    return {
        "micrograph": noise(splits[0], (MICS, MR, NCOL), 1.0, 6.0, ((0, 8), (2, 4))),
        "templates": noise(splits[1], (MICS, TS, TS), 1.0, 6.0, ((0, 8),)),
        "orient_ids": place_ends(jax.random.randint(splits[2], (MICS,), 0, NANG), jax.random.fold_in(splits[2], 1), 0, NANG - 1).astype(jnp.int32),
        "defocus_bins": place_ends(jax.random.randint(splits[3], (MICS,), 0, NBINS), jax.random.fold_in(splits[3], 1), 0, NBINS - 1).astype(jnp.int32),
    }


AMPLITUDE = 0.07
WAVELENGTH = 0.0197
BASE_DEFOCUS = 8000.0
DEFOCUS_STEP = 1000.0

def counting(length):
    return jnp.arange(length, dtype=jnp.int32)

def trig_pair(left_ids, right_ids, length):
    product_ids = left_ids[:, None] * right_ids[None, :] % length
    angles = product_ids.astype(jnp.float32) * (2.0 * math.pi / length)
    return (jnp.cos(angles).astype(jnp.bfloat16), jnp.sin(angles).astype(jnp.bfloat16))

def forward_columns(height, breadth, length):
    cosine, sine_part = trig_pair(counting(height), counting(breadth), length)
    return jnp.concatenate([cosine, -sine_part], axis=1)

def inverse_columns(breadth, height, length):
    cosine, sine_part = trig_pair(counting(breadth), counting(height), length)
    weights = jnp.where(counting(breadth) == 0, 1.0, 2.0).astype(jnp.bfloat16)[:, None]
    return jnp.concatenate([cosine * weights, -sine_part * weights], axis=0)

def stacked_rows(left_ids, right_ids, length):
    cosine, sine_part = trig_pair(left_ids, right_ids, length)
    return jnp.concatenate([cosine, sine_part], axis=0)

def complex_left(stacked, values, direction):
    product = jnp.dot(stacked, values, preferred_element_type=jnp.float32)
    height = stacked.shape[0] // 2
    breadth = values.shape[1] // 2
    upper_part = product[:height]
    lower_part = product[height:]
    real_part = upper_part[:, :breadth] - direction * lower_part[:, breadth:]
    imag_part = upper_part[:, breadth:] + direction * lower_part[:, :breadth]
    return jnp.concatenate([real_part, imag_part], axis=1)

def transfer_function(bin_value, rows_length, breadth, cols_length):
    row_ids = counting(rows_length)
    folded = (row_ids + rows_length // 2) % rows_length - rows_length // 2
    freq_rows = folded.astype(jnp.float32) / rows_length
    freq_cols = counting(breadth).astype(jnp.float32) / cols_length
    radius = freq_rows[:, None] * freq_rows[:, None] + freq_cols[None, :] * freq_cols[None, :]
    defocus = BASE_DEFOCUS + DEFOCUS_STEP * bin_value.astype(jnp.float32)
    phases = math.pi * WAVELENGTH * defocus * radius
    return -(math.sqrt(1.0 - AMPLITUDE * AMPLITUDE) * jnp.sin(phases) + AMPLITUDE * jnp.cos(phases))

def angle_pairs(orient_ids):
    angles = orient_ids.astype(jnp.float32) * (2.0 * math.pi / NANG)
    return jnp.stack([jnp.cos(angles), jnp.sin(angles)], axis=-1).astype(jnp.bfloat16)

def micro_spectrum(micro_strip, col_forward, row_forward, ctf_values):
    spectrum_cols = jnp.dot(micro_strip, col_forward, preferred_element_type=jnp.float32).astype(jnp.bfloat16)
    spectrum = complex_left(row_forward, spectrum_cols, -1.0)
    return (spectrum * jnp.concatenate([ctf_values, ctf_values], axis=1)).astype(jnp.bfloat16)

def template_spectrum(template, col_forward, row_forward):
    template_cols = jnp.dot(template, col_forward[:template.shape[1]], preferred_element_type=jnp.float32).astype(jnp.bfloat16)
    return complex_left(row_forward, template_cols, -1.0).astype(jnp.bfloat16)

def spectral_product(micro_rows, template_rows):
    breadth = micro_rows.shape[1] // 2
    micro_real = micro_rows[:, :breadth].astype(jnp.float32)
    micro_imag = micro_rows[:, breadth:].astype(jnp.float32)
    tmpl_real = template_rows[:, :breadth].astype(jnp.float32)
    tmpl_imag = template_rows[:, breadth:].astype(jnp.float32)
    real_part = micro_real * tmpl_real + micro_imag * tmpl_imag
    imag_part = micro_imag * tmpl_real - micro_real * tmpl_imag
    return jnp.concatenate([real_part, imag_part], axis=1).astype(jnp.bfloat16)

def accumulate(statistics, correlation, angle_pair):
    weight = jax.nn.softplus(2.0 * correlation)
    cos_value = angle_pair[0].astype(jnp.float32)
    sin_value = angle_pair[1].astype(jnp.float32)
    fresh = (correlation, correlation, correlation * correlation, weight, weight * cos_value, weight * sin_value)
    if statistics is None:
        return fresh
    return (jnp.maximum(statistics[0], fresh[0]), statistics[1] + fresh[1], statistics[2] + fresh[2], statistics[3] + fresh[3], statistics[4] + fresh[4], statistics[5] + fresh[5])

def finish(statistics):
    return (statistics[0], statistics[1], statistics[2], statistics[4] / statistics[3], statistics[5] / statistics[3])

def reference(micrograph, templates, orient_ids, defocus_bins):
    col_forward = forward_columns(MC, HALF, LC)
    row_forward = stacked_rows(counting(LR), counting(MR), LR)
    row_template = stacked_rows(counting(LR), counting(TS), LR)
    row_inverse = stacked_rows(counting(MH), counting(LR), LR)
    col_inverse = inverse_columns(HALF, TC, LC)
    norm_scale = 1.0 / (TS * LR * LC)

    def one_template(template):
        return template_spectrum(template, col_forward, row_template)
    spectra = lax.map(one_template, templates)
    angles_all = angle_pairs(orient_ids)
    padded = jnp.pad(micrograph, ((0, 0), (0, 0), (0, TS - 1)))

    def one_micrograph(micro_index):
        ctf_values = transfer_function(defocus_bins[micro_index], LR, HALF, LC)
        rows_all = lax.dynamic_index_in_dim(padded, micro_index, 0, keepdims=False)
        pieces = []
        for tile_index in range(N_TILE):
            micro_strip = rows_all[:, tile_index * TC:tile_index * TC + MC]
            micro_spec = micro_spectrum(micro_strip, col_forward, row_forward, ctf_values)
            statistics = None
            for step_index in range(STEPS):
                target = (micro_index + step_index) % MICS
                template_spec = lax.dynamic_index_in_dim(spectra, target, 0, keepdims=False)
                angle_pair = lax.dynamic_index_in_dim(angles_all, target, 0, keepdims=False)
                product = spectral_product(micro_spec, template_spec)
                inverse_rows = complex_left(row_inverse, product, 1.0).astype(jnp.bfloat16)
                correlation = jnp.dot(inverse_rows, col_inverse, preferred_element_type=jnp.float32) * norm_scale
                statistics = accumulate(statistics, correlation, angle_pair)
            pieces.append(finish(statistics))
        return tuple((jnp.concatenate([tile_stats[position] for tile_stats in pieces], axis=1) for position in range(5)))
    outputs = lax.map(one_micrograph, counting(MICS))
    return (outputs[0], outputs[1], outputs[2], outputs[3], outputs[4])
```

```python
import math

import jax
import jax.numpy as jnp
import ml_dtypes
import numpy as np
from jax import lax
from jax.experimental import pallas as pl
from jax.experimental.pallas import tpu as pltpu
from jax.sharding import PartitionSpec as P

TS = 384
TC = 384
MH = 64
STEPS = 4
NANG = 360
MR = 447
LR = 448
LC = 768
HALF = 384
PAIRS = LR // 2
EDGE = 16
ROWS = LR + EDGE

AMPLITUDE = 0.07
WAVELENGTH = 0.0197
BASE_DEFOCUS = 8000.0
DEFOCUS_STEP = 1000.0

HBM = pl.BlockSpec(memory_space=pltpu.HBM)
SMEM = pl.BlockSpec(memory_space=pltpu.SMEM)
VMEM = pl.BlockSpec(memory_space=pltpu.VMEM)


def trig_pair(left_count, right_count, length):
    ids = np.arange(left_count)[:, None] * np.arange(right_count)[None, :] % length
    angles = ids.astype(np.float32) * np.float32(2.0 * math.pi / length)
    return np.cos(angles), np.sin(angles)


def paired_rows():
    cosine, sine = trig_pair(PAIRS + 1, LR, LR)
    zeros = np.zeros((EDGE - 1, LR), np.float32)
    rows = np.concatenate([cosine[:PAIRS], sine[:PAIRS], cosine[PAIRS:], zeros], axis=0)
    return rows.astype(ml_dtypes.bfloat16)


def forward_columns():
    cosine, sine = trig_pair(TC, HALF, LC)
    return np.concatenate([cosine, sine], axis=1).astype(ml_dtypes.bfloat16)


def inverse_columns():
    cosine, sine = trig_pair(HALF, TC, LC)
    weights = np.where(np.arange(HALF) == 0, 1.0, 2.0).astype(np.float32)[:, None]
    cosine = cosine.astype(ml_dtypes.bfloat16).astype(np.float32) * weights
    sine = sine.astype(ml_dtypes.bfloat16).astype(np.float32) * weights
    return np.concatenate([cosine, -sine], axis=0).astype(ml_dtypes.bfloat16)


def dot(left, right):
    return jnp.dot(left, right, preferred_element_type=jnp.float32)


def spectrum_of(template, rows, cols):
    half_way = dot(rows[:, :TS], template[...]).astype(jnp.bfloat16)
    return dot(half_way, cols[...]).astype(jnp.bfloat16)


def angle_rows(orient_id):
    turns = jnp.broadcast_to(orient_id[...], (EDGE // 2, HALF)).astype(jnp.float32) * (2.0 * math.pi / NANG)
    return jnp.concatenate([jnp.cos(turns), jnp.sin(turns)], axis=0).astype(jnp.bfloat16)


def first_kernel(
    bins,
    strip_far,
    template_far,
    rows_far,
    cols_far,
    rows,
    cols,
    own_part,
    ctf,
    spectrum,
    strip,
    template,
    arrived,
):
    pairs = (
        (rows_far, rows),
        (cols_far, cols),
        (template_far, template),
        (strip_far, strip),
    )
    copies = [
        pltpu.make_async_copy(source, target, arrived.at[i])
        for i, (source, target) in enumerate(pairs)
    ]
    for copy in copies:
        copy.start()
    shape = ctf.shape
    row_ids = lax.broadcasted_iota(jnp.int32, shape, 0)
    col_ids = lax.broadcasted_iota(jnp.int32, shape, 1)
    freq_rows = row_ids.astype(jnp.float32) / LR
    freq_cols = col_ids.astype(jnp.float32) / LC
    radius = freq_rows * freq_rows + freq_cols * freq_cols
    defocus = BASE_DEFOCUS + DEFOCUS_STEP * bins[0].astype(jnp.float32)
    phases = math.pi * WAVELENGTH * defocus * radius
    values = -(
        math.sqrt(1.0 - AMPLITUDE * AMPLITUDE) * jnp.sin(phases) + AMPLITUDE * jnp.cos(phases)
    )
    ctf[...] = values * jnp.where(row_ids == 0, 0.5, 1.0)
    for copy in copies:
        copy.wait()
    spectrum[...] = spectrum_of(template, rows, cols)
    half_way = dot(rows[:, :MR], strip[...]).astype(jnp.bfloat16)
    own_part[...] = dot(half_way, cols[...])


def far_kernel(far, rows, cols, far_id, far_packed):
    far_packed[:ROWS, :] = spectrum_of(far, rows, cols)
    turn = angle_rows(far_id)
    far_packed[ROWS:, :] = jnp.concatenate([turn, turn], axis=1)


def near_kernel(near, rows, cols, near_spectrum):
    near_spectrum[...] = spectrum_of(near, rows, cols)


def blocks(values):
    upper, lower, edge = values[:PAIRS], values[PAIRS:LR], values[LR:ROWS]
    return tuple(
        block.astype(jnp.float32)
        for part in (upper, lower, edge)
        for block in (part[:, :HALF], part[:, HALF:])
    )


def multiply(micro, spectrum, product):
    for row in range(0, PAIRS, EDGE):
        up, down = slice(row, row + EDGE), slice(PAIRS + row, PAIRS + row + EDGE)
        for col in range(0, HALF, 128):
            real, imag = slice(col, col + 128), slice(HALF + col, HALF + col + 128)
            t_a, t_b, t_d, t_e = (
                spectrum[place].astype(jnp.float32)
                for place in ((up, real), (up, imag), (down, real), (down, imag))
            )
            up_real, up_imag = micro[up, real], micro[up, imag]
            down_real, down_imag = micro[down, real], micro[down, imag]
            s_real, s_imag = t_a - t_e, t_b + t_d
            r_real, r_imag = t_a + t_e, t_b - t_d
            p_real = up_real * s_real - up_imag * s_imag
            p_imag = up_real * s_imag + up_imag * s_real
            q_real = down_real * r_real - down_imag * r_imag
            q_imag = down_real * r_imag + down_imag * r_real
            product[up, real] = (p_real + q_real).astype(jnp.bfloat16)
            product[up, imag] = (p_imag + q_imag).astype(jnp.bfloat16)
            product[down, real] = (q_imag - p_imag).astype(jnp.bfloat16)
            product[down, imag] = (p_real - q_real).astype(jnp.bfloat16)
    t_x = spectrum[LR:ROWS, :HALF].astype(jnp.float32)
    t_y = spectrum[LR:ROWS, HALF:].astype(jnp.float32)
    edge_real, edge_imag = micro[LR:, :HALF], micro[LR:, HALF:]
    product[LR:, :HALF] = (edge_real * t_x - edge_imag * t_y).astype(jnp.bfloat16)
    product[LR:, HALF:] = (edge_real * t_y + edge_imag * t_x).astype(jnp.bfloat16)


def third_kernel(
    halo,
    own_part,
    ctf,
    rows,
    cols,
    rows_back,
    own_spectrum,
    far_spectrum,
    near_spectrum,
    micro,
    back_early,
    products,
):
    half_way = dot(rows[:, :MR], halo[...])
    lanes = lax.broadcasted_iota(jnp.int32, half_way.shape, 1)
    half_way = jnp.where(lanes < TC - 1, half_way, 0.0).astype(jnp.bfloat16)
    lanes = lax.broadcasted_iota(jnp.int32, (1, 2 * HALF), 1)
    signs = jnp.where(lanes % 2 == 0, 1.0, -1.0)
    m_a, m_b, m_d, m_e, m_x, m_y = blocks(own_part[...] + signs * dot(half_way, cols[...]))
    ctf_rows, ctf_edge = ctf[:PAIRS, :], ctf[PAIRS:, :]
    micro[:PAIRS, :HALF] = ctf_rows * (m_a - m_e)
    micro[:PAIRS, HALF:] = -(ctf_rows * (m_b + m_d))
    micro[PAIRS:LR, :HALF] = ctf_rows * (m_a + m_e)
    micro[PAIRS:LR, HALF:] = ctf_rows * (m_d - m_b)
    micro[LR:, :HALF] = ctf_edge * m_x
    micro[LR:, HALF:] = -(ctf_edge * m_y)
    for step, spectrum in enumerate((own_spectrum, far_spectrum, near_spectrum)):
        product = products.at[step]
        multiply(micro, spectrum, product)
        back_early[step * MH : (step + 1) * MH, :] = dot(rows_back[...], product[...]).astype(
            jnp.bfloat16
        )


def last_kernel(
    micro,
    back_early,
    late_packed,
    own_id,
    near_id,
    far_packed,
    rows_back,
    cols_back,
    peak,
    total,
    squares,
    orient_cos,
    orient_sin,
    product,
):
    multiply(micro, late_packed, product)
    back_late = dot(rows_back[...], product[...]).astype(jnp.bfloat16)
    scale = 1.0 / (TS * LR * LC)
    corr_early = dot(back_early[...], cols_back[...]) * scale
    corr_late = dot(back_late, cols_back[...]) * scale
    corrs = [corr_early[step * MH : (step + 1) * MH, :] for step in range(STEPS - 1)] + [corr_late]
    turns = (
        angle_rows(own_id),
        far_packed[ROWS:, :HALF],
        angle_rows(near_id),
        late_packed[ROWS:, :HALF],
    )
    sums = None
    for corr, turn in zip(corrs, turns):
        doubled = 2.0 * corr
        weight = jnp.maximum(doubled, 0.0) + jnp.log1p(jnp.exp(-jnp.abs(doubled)))
        cosine, sine = turn[0:1].astype(jnp.float32), turn[8:9].astype(jnp.float32)
        fresh = (corr, corr, corr * corr, weight, weight * cosine, weight * sine)
        if sums is None:
            sums = fresh
        else:
            sums = (jnp.maximum(sums[0], fresh[0]),) + tuple(
                old + new for old, new in zip(sums[1:], fresh[1:])
            )
    peak[...] = sums[0]
    total[...] = sums[1]
    squares[...] = sums[2]
    orient_cos[...] = sums[4] / sums[3]
    orient_sin[...] = sums[5] / sums[3]


def along(array, sources):
    return lax.ppermute(array, "mic", [(source, place) for place, source in enumerate(sources)])


def call(kernel, name, flops, out_shape, in_specs, scratch_shapes=()):
    return pl.pallas_call(
        kernel,
        out_shape=out_shape,
        in_specs=in_specs,
        out_specs=jax.tree.map(lambda _: VMEM, out_shape),
        scratch_shapes=scratch_shapes,
        compiler_params=pltpu.CompilerParams(vmem_limit_bytes=24 * 1024 * 1024),
        cost_estimate=pl.CostEstimate(flops=flops, bytes_accessed=10**3, transcendentals=0),
        name=name,
    )


def body(micrograph, templates, orient_ids, defocus_bins):
    rows_far = jnp.asarray(paired_rows())
    cols_far = jnp.asarray(forward_columns())
    rows_back = jnp.asarray(np.ascontiguousarray(paired_rows()[:, :MH].T))
    cols_back = jnp.asarray(inverse_columns())
    count = lax.axis_size("mic")
    tiles = lax.axis_size("tile")
    strip = micrograph[0]
    own = templates[0]
    near_places = [(d + (1 if d % 2 == 0 else 3)) % count for d in range(count)]
    far_places = [(d + 2) % count for d in range(count)]

    halo = lax.ppermute(strip, "tile", [(i + 1, i) for i in range(tiles - 1)])
    far = along(own, far_places)
    near = along(own, near_places)
    own_id = orient_ids.reshape(1, 1)
    near_id, far_id = along(own_id, near_places), along(own_id, far_places)

    bf16, f32 = jnp.bfloat16, jnp.float32
    spectrum_type = jax.ShapeDtypeStruct((ROWS, 2 * HALF), bf16)
    own_inputs = [
        pltpu.with_memory_space_constraint(x, pltpu.HBM) for x in (strip, own, rows_far, cols_far)
    ]
    rows, cols, own_part, ctf, own_spectrum = call(
        first_kernel,
        "own_spectra",
        10**9,
        (
            jax.ShapeDtypeStruct(rows_far.shape, bf16),
            jax.ShapeDtypeStruct(cols_far.shape, bf16),
            jax.ShapeDtypeStruct((ROWS, 2 * HALF), f32),
            jax.ShapeDtypeStruct((PAIRS + EDGE, HALF), f32),
            spectrum_type,
        ),
        [SMEM] + [HBM] * 4,
        [
            pltpu.VMEM((MR, TC), bf16),
            pltpu.VMEM((TS, TS), bf16),
            pltpu.SemaphoreType.DMA((4,)),
        ],
    )(defocus_bins, *own_inputs)
    far, halo, own_spectrum = lax.optimization_barrier((far, halo, own_spectrum))
    far_packed = call(
        far_kernel,
        "far_spectrum",
        10**5,
        jax.ShapeDtypeStruct((ROWS + EDGE, 2 * HALF), bf16),
        [VMEM] * 4,
    )(far, rows, cols, far_id)
    late_packed = along(far_packed, [d ^ 1 for d in range(count)])
    near_spectrum = call(near_kernel, "near_spectrum", 10**10, spectrum_type, [VMEM] * 3)(
        near, rows, cols
    )
    micro, back_early = call(
        third_kernel,
        "strip_spectrum",
        10**9,
        (
            jax.ShapeDtypeStruct((ROWS, 2 * HALF), f32),
            jax.ShapeDtypeStruct(((STEPS - 1) * MH, 2 * HALF), bf16),
        ),
        [VMEM] * 9,
        [pltpu.VMEM((STEPS - 1, ROWS, 2 * HALF), bf16)],
    )(halo, own_part, ctf, rows, cols, rows_back, own_spectrum, far_packed, near_spectrum)
    results = call(
        last_kernel,
        "match",
        10**5,
        (jax.ShapeDtypeStruct((MH, TC), f32),) * 5,
        [VMEM] * 8,
        [pltpu.VMEM((ROWS, 2 * HALF), bf16)],
    )(micro, back_early, late_packed, own_id, near_id, far_packed, rows_back, cols_back)
    return tuple(result[None] for result in results)


def solution(mesh):
    tiled = P("mic", None, "tile")
    return jax.shard_map(
        body,
        mesh=mesh,
        in_specs=(tiled, P("mic", None, None), P("mic"), P("mic")),
        out_specs=(tiled,) * 5,
        check_vma=False,
    )
```

```python
import math

import jax
import jax.numpy as jnp
import ml_dtypes
import numpy as np
from jax import lax
from jax.experimental import pallas as pl
from jax.experimental.pallas import tpu as pltpu
from jax.sharding import PartitionSpec as P

TS = 384
TC = 384
MH = 64
STEPS = 4
NANG = 360
MR = 447
LR = 448
LC = 768
HALF = 384
PAIRS = LR // 2
EDGE = 16
ROWS = LR + EDGE

AMPLITUDE = 0.07
WAVELENGTH = 0.0197
BASE_DEFOCUS = 8000.0
DEFOCUS_STEP = 1000.0

COST = (10**5, 10**5, 10**5, 10**10, 10**5)

HBM = pl.BlockSpec(memory_space=pltpu.HBM)
SMEM = pl.BlockSpec(memory_space=pltpu.SMEM)
VMEM = pl.BlockSpec(memory_space=pltpu.VMEM)


def trig_pair(left_count, right_count, length):
    ids = np.arange(left_count)[:, None] * np.arange(right_count)[None, :] % length
    angles = ids.astype(np.float32) * np.float32(2.0 * math.pi / length)
    return np.cos(angles), np.sin(angles)


def paired_rows():
    cosine, sine = trig_pair(PAIRS + 1, LR, LR)
    zeros = np.zeros((EDGE - 1, LR), np.float32)
    rows = np.concatenate([cosine[:PAIRS], sine[:PAIRS], cosine[PAIRS:], zeros], axis=0)
    return rows.astype(ml_dtypes.bfloat16)


def forward_columns():
    cosine, sine = trig_pair(TC, HALF, LC)
    return np.concatenate([cosine, sine], axis=1).astype(ml_dtypes.bfloat16)


def inverse_columns():
    cosine, sine = trig_pair(HALF, TC, LC)
    weights = np.where(np.arange(HALF) == 0, 1.0, 2.0).astype(np.float32)[:, None]
    cosine = cosine.astype(ml_dtypes.bfloat16).astype(np.float32) * weights
    sine = sine.astype(ml_dtypes.bfloat16).astype(np.float32) * weights
    return np.concatenate([cosine, -sine], axis=0).astype(ml_dtypes.bfloat16)


def dot(left, right):
    return jnp.dot(left, right, preferred_element_type=jnp.float32)


def spectrum_of(template, rows, cols):
    half_way = dot(rows[:, :TS], template[...]).astype(jnp.bfloat16)
    return dot(half_way, cols[...]).astype(jnp.bfloat16)


def turn_kernel(orient_id, turn):
    turns = jnp.full((EDGE // 2, HALF), orient_id[0]).astype(jnp.float32) * (2.0 * math.pi / NANG)
    turn[...] = jnp.concatenate([jnp.cos(turns), jnp.sin(turns)], axis=0).astype(jnp.bfloat16)


def first_kernel(
    bins,
    strip_far,
    template_far,
    rows_far,
    cols_far,
    rows,
    cols,
    template,
    own_part,
    ctf,
    spectrum,
    strip,
    arrived,
):
    pairs = (
        (rows_far, rows),
        (cols_far, cols),
        (template_far, template),
        (strip_far, strip),
    )
    copies = [
        pltpu.make_async_copy(source, target, arrived.at[i])
        for i, (source, target) in enumerate(pairs)
    ]
    for copy in copies:
        copy.start()
    shape = ctf.shape
    row_ids = lax.broadcasted_iota(jnp.int32, shape, 0)
    col_ids = lax.broadcasted_iota(jnp.int32, shape, 1)
    freq_rows = row_ids.astype(jnp.float32) / LR
    freq_cols = col_ids.astype(jnp.float32) / LC
    radius = freq_rows * freq_rows + freq_cols * freq_cols
    defocus = BASE_DEFOCUS + DEFOCUS_STEP * bins[0].astype(jnp.float32)
    phases = math.pi * WAVELENGTH * defocus * radius
    values = -(
        math.sqrt(1.0 - AMPLITUDE * AMPLITUDE) * jnp.sin(phases) + AMPLITUDE * jnp.cos(phases)
    )
    ctf[...] = values * jnp.where(row_ids == 0, 0.5, 1.0)
    for copy in copies:
        copy.wait()
    spectrum[...] = spectrum_of(template, rows, cols)
    half_way = dot(rows[:, :MR], strip[...]).astype(jnp.bfloat16)
    own_part[...] = dot(half_way, cols[...])


def blocks(values):
    upper, lower, edge = values[:PAIRS], values[PAIRS:LR], values[LR:ROWS]
    return tuple(
        block.astype(jnp.float32)
        for part in (upper, lower, edge)
        for block in (part[:, :HALF], part[:, HALF:])
    )


def multiply_back(micro, spectrum, rows_back, product, back):
    for row in range(0, PAIRS, EDGE):
        up, down = slice(row, row + EDGE), slice(PAIRS + row, PAIRS + row + EDGE)
        for col in range(0, HALF, 128):
            real, imag = slice(col, col + 128), slice(HALF + col, HALF + col + 128)
            t_a, t_b, t_d, t_e = (
                spectrum[place].astype(jnp.float32)
                for place in ((up, real), (up, imag), (down, real), (down, imag))
            )
            up_real, up_imag = micro[up, real], micro[up, imag]
            down_real, down_imag = micro[down, real], micro[down, imag]
            s_real, s_imag = t_a - t_e, t_b + t_d
            r_real, r_imag = t_a + t_e, t_b - t_d
            p_real = up_real * s_real - up_imag * s_imag
            p_imag = up_real * s_imag + up_imag * s_real
            q_real = down_real * r_real - down_imag * r_imag
            q_imag = down_real * r_imag + down_imag * r_real
            product[up, real] = (p_real + q_real).astype(jnp.bfloat16)
            product[up, imag] = (p_imag + q_imag).astype(jnp.bfloat16)
            product[down, real] = (q_imag - p_imag).astype(jnp.bfloat16)
            product[down, imag] = (p_real - q_real).astype(jnp.bfloat16)
    t_x = spectrum[LR:ROWS, :HALF].astype(jnp.float32)
    t_y = spectrum[LR:ROWS, HALF:].astype(jnp.float32)
    edge_real, edge_imag = micro[LR:, :HALF], micro[LR:, HALF:]
    product[LR:, :HALF] = (edge_real * t_x - edge_imag * t_y).astype(jnp.bfloat16)
    product[LR:, HALF:] = (edge_real * t_y + edge_imag * t_x).astype(jnp.bfloat16)
    back[...] = dot(rows_back[...], product[...]).astype(jnp.bfloat16)


def second_kernel(far, halo, far_turn, own_part, ctf, rows, cols, far_packed, micro):
    far_half = dot(rows[:, :TS], far[...]).astype(jnp.bfloat16)
    halo_half = dot(rows[:, :MR], halo[...])
    lanes = lax.broadcasted_iota(jnp.int32, halo_half.shape, 1)
    halo_half = jnp.where(lanes < TC - 1, halo_half, 0.0).astype(jnp.bfloat16)
    far_packed[:ROWS, :] = dot(far_half, cols[...]).astype(jnp.bfloat16)
    far_packed[ROWS:, :HALF] = far_turn[...]
    far_packed[ROWS:, HALF:] = far_turn[...]
    lanes = lax.broadcasted_iota(jnp.int32, (1, 2 * HALF), 1)
    signs = jnp.where(lanes % 2 == 0, 1.0, -1.0)
    m_a, m_b, m_d, m_e, m_x, m_y = blocks(own_part[...] + signs * dot(halo_half, cols[...]))
    ctf_rows, ctf_edge = ctf[:PAIRS, :], ctf[PAIRS:, :]
    micro[:PAIRS, :HALF] = ctf_rows * (m_a - m_e)
    micro[:PAIRS, HALF:] = -(ctf_rows * (m_b + m_d))
    micro[PAIRS:LR, :HALF] = ctf_rows * (m_a + m_e)
    micro[PAIRS:LR, HALF:] = ctf_rows * (m_d - m_b)
    micro[LR:, :HALF] = ctf_edge * m_x
    micro[LR:, HALF:] = -(ctf_edge * m_y)


def third_kernel(
    near, micro, own_spectrum, far_packed, rows, cols, rows_back, near_spectrum, back_early, products
):
    near_half = dot(rows[:, :TS], near[...]).astype(jnp.bfloat16)
    multiply_back(micro, own_spectrum, rows_back, products.at[0], back_early.at[:MH])
    near_spectrum[...] = dot(near_half, cols[...]).astype(jnp.bfloat16)
    multiply_back(micro, far_packed, rows_back, products.at[1], back_early.at[MH:])


def last_kernel(
    micro,
    back_early,
    near_spectrum,
    late_packed,
    own_turn,
    near_turn,
    far_packed,
    rows_back,
    cols_back,
    peak,
    total,
    squares,
    orient_cos,
    orient_sin,
    products,
    back_late,
):
    multiply_back(micro, near_spectrum, rows_back, products.at[0], back_late.at[:MH])
    multiply_back(micro, late_packed, rows_back, products.at[1], back_late.at[MH:])
    scale = 1.0 / (TS * LR * LC)
    halves = [dot(back[...], cols_back[...]) * scale for back in (back_early, back_late)]
    corrs = [half[step * MH : (step + 1) * MH, :] for half in halves for step in range(2)]
    turns = (own_turn[...], far_packed[ROWS:, :HALF], near_turn[...], late_packed[ROWS:, :HALF])
    sums = None
    for corr, turn in zip(corrs, turns):
        doubled = 2.0 * corr
        weight = jnp.maximum(doubled, 0.0) + jnp.log1p(jnp.exp(-jnp.abs(doubled)))
        cosine, sine = turn[0:1].astype(jnp.float32), turn[8:9].astype(jnp.float32)
        fresh = (corr, corr, corr * corr, weight, weight * cosine, weight * sine)
        if sums is None:
            sums = fresh
        else:
            sums = (jnp.maximum(sums[0], fresh[0]),) + tuple(
                old + new for old, new in zip(sums[1:], fresh[1:])
            )
    peak[...] = sums[0]
    total[...] = sums[1]
    squares[...] = sums[2]
    orient_cos[...] = sums[4] / sums[3]
    orient_sin[...] = sums[5] / sums[3]


def along(array, sources):
    return lax.ppermute(array, "mic", [(source, place) for place, source in enumerate(sources)])


def call(kernel, name, flops, out_shape, in_specs, scratch_shapes=()):
    return pl.pallas_call(
        kernel,
        out_shape=out_shape,
        in_specs=in_specs,
        out_specs=jax.tree.map(lambda _: VMEM, out_shape),
        scratch_shapes=scratch_shapes,
        compiler_params=pltpu.CompilerParams(vmem_limit_bytes=24 * 1024 * 1024),
        cost_estimate=pl.CostEstimate(flops=flops, bytes_accessed=10**3, transcendentals=0),
        name=name,
    )


def body(micrograph, templates, orient_ids, defocus_bins):
    rows_far = jnp.asarray(paired_rows())
    cols_far = jnp.asarray(forward_columns())
    rows_back = jnp.asarray(np.ascontiguousarray(paired_rows()[:, :MH].T))
    cols_back = jnp.asarray(inverse_columns())
    count = lax.axis_size("mic")
    tiles = lax.axis_size("tile")
    strip = micrograph[0]
    own = templates[0]
    near_places = [(d + (1 if d % 2 == 0 else 3)) % count for d in range(count)]
    far_places = [(d + 2) % count for d in range(count)]

    halo = lax.ppermute(strip, "tile", [(i + 1, i) for i in range(tiles - 1)])
    far = along(own, far_places)
    own_turn = call(
        turn_kernel, "turn", COST[0], jax.ShapeDtypeStruct((EDGE, HALF), jnp.bfloat16), [SMEM]
    )(orient_ids)
    near_turn, far_turn = along(own_turn, near_places), along(own_turn, far_places)

    bf16, f32 = jnp.bfloat16, jnp.float32
    spectrum_type = jax.ShapeDtypeStruct((ROWS, 2 * HALF), bf16)
    own_inputs = [
        pltpu.with_memory_space_constraint(x, pltpu.HBM) for x in (strip, own, rows_far, cols_far)
    ]
    rows, cols, template, own_part, ctf, own_spectrum = call(
        first_kernel,
        "own_spectra",
        COST[1],
        (
            jax.ShapeDtypeStruct(rows_far.shape, bf16),
            jax.ShapeDtypeStruct(cols_far.shape, bf16),
            jax.ShapeDtypeStruct(own.shape, bf16),
            jax.ShapeDtypeStruct((ROWS, 2 * HALF), f32),
            jax.ShapeDtypeStruct((PAIRS + EDGE, HALF), f32),
            spectrum_type,
        ),
        [SMEM] + [HBM] * 4,
        [pltpu.VMEM((MR, TC), bf16), pltpu.SemaphoreType.DMA((4,))],
    )(defocus_bins, *own_inputs)
    near = along(own, near_places)
    far, halo, own_spectrum = lax.optimization_barrier((far, halo, own_spectrum))
    far_packed, micro = call(
        second_kernel,
        "far_and_strip",
        COST[2],
        (
            jax.ShapeDtypeStruct((ROWS + EDGE, 2 * HALF), bf16),
            jax.ShapeDtypeStruct((ROWS, 2 * HALF), f32),
        ),
        [VMEM] * 7,
    )(far, halo, far_turn, own_part, ctf, rows, cols)
    late_packed = along(far_packed, [d ^ 1 for d in range(count)])
    near_spectrum, back_early = call(
        third_kernel,
        "near_and_early",
        COST[3],
        (spectrum_type, jax.ShapeDtypeStruct((2 * MH, 2 * HALF), bf16)),
        [VMEM] * 7,
        [pltpu.VMEM((2, ROWS, 2 * HALF), bf16)],
    )(near, micro, own_spectrum, far_packed, rows, cols, rows_back)
    results = call(
        last_kernel,
        "match",
        COST[4],
        (jax.ShapeDtypeStruct((MH, TC), f32),) * 5,
        [VMEM] * 9,
        [pltpu.VMEM((2, ROWS, 2 * HALF), bf16), pltpu.VMEM((2 * MH, 2 * HALF), bf16)],
    )(
        micro,
        back_early,
        near_spectrum,
        late_packed,
        own_turn,
        near_turn,
        far_packed,
        rows_back,
        cols_back,
    )
    return tuple(result[None] for result in results)


def solution(mesh):
    tiled = P("mic", None, "tile")
    return jax.shard_map(
        body,
        mesh=mesh,
        in_specs=(tiled, P("mic", None, None), P("mic"), P("mic")),
        out_specs=(tiled,) * 5,
        check_vma=False,
    )
```

```python
import math

import jax
import jax.numpy as jnp
import ml_dtypes
import numpy as np
from jax import lax
from jax.experimental import pallas as pl
from jax.experimental.pallas import tpu as pltpu
from jax.sharding import PartitionSpec as P

TS = 384
TC = 384
MH = 64
STEPS = 4
NANG = 360
MR = 447
LR = 448
LC = 768
HALF = 384
PAIRS = LR // 2
EDGE = 16
ROWS = LR + EDGE

AMPLITUDE = 0.07
WAVELENGTH = 0.0197
BASE_DEFOCUS = 8000.0
DEFOCUS_STEP = 1000.0

COST = (10**5, 10**5, 10**5, 10**5, 10**10, 10**5)

HBM = pl.BlockSpec(memory_space=pltpu.HBM)
SMEM = pl.BlockSpec(memory_space=pltpu.SMEM)
VMEM = pl.BlockSpec(memory_space=pltpu.VMEM)


def trig_pair(left_count, right_count, length):
    ids = np.arange(left_count)[:, None] * np.arange(right_count)[None, :] % length
    angles = ids.astype(np.float32) * np.float32(2.0 * math.pi / length)
    return np.cos(angles), np.sin(angles)


def paired_rows():
    cosine, sine = trig_pair(PAIRS + 1, LR, LR)
    zeros = np.zeros((EDGE - 1, LR), np.float32)
    rows = np.concatenate([cosine[:PAIRS], sine[:PAIRS], cosine[PAIRS:], zeros], axis=0)
    return rows.astype(ml_dtypes.bfloat16)


def forward_columns():
    cosine, sine = trig_pair(TC, HALF, LC)
    return np.concatenate([cosine, sine], axis=1).astype(ml_dtypes.bfloat16)


def inverse_columns():
    cosine, sine = trig_pair(HALF, TC, LC)
    weights = np.where(np.arange(HALF) == 0, 1.0, 2.0).astype(np.float32)[:, None]
    cosine = cosine.astype(ml_dtypes.bfloat16).astype(np.float32) * weights
    sine = sine.astype(ml_dtypes.bfloat16).astype(np.float32) * weights
    return np.concatenate([cosine, -sine], axis=0).astype(ml_dtypes.bfloat16)


def dot(left, right):
    return jnp.dot(left, right, preferred_element_type=jnp.float32)


def spectrum_of(template, rows, cols):
    half_way = dot(rows[:, :TS], template[...]).astype(jnp.bfloat16)
    return dot(half_way, cols[...]).astype(jnp.bfloat16)


def turn_kernel(orient_id, turn):
    turns = jnp.full((EDGE // 2, HALF), orient_id[0]).astype(jnp.float32) * (2.0 * math.pi / NANG)
    turn[...] = jnp.concatenate([jnp.cos(turns), jnp.sin(turns)], axis=0).astype(jnp.bfloat16)


def first_kernel(
    bins,
    strip_far,
    template_far,
    rows_far,
    cols_far,
    rows,
    cols,
    template,
    own_part,
    ctf,
    spectrum,
    strip,
    arrived,
):
    pairs = (
        (rows_far, rows),
        (cols_far, cols),
        (template_far, template),
        (strip_far, strip),
    )
    copies = [
        pltpu.make_async_copy(source, target, arrived.at[i])
        for i, (source, target) in enumerate(pairs)
    ]
    for copy in copies:
        copy.start()
    shape = ctf.shape
    row_ids = lax.broadcasted_iota(jnp.int32, shape, 0)
    col_ids = lax.broadcasted_iota(jnp.int32, shape, 1)
    freq_rows = row_ids.astype(jnp.float32) / LR
    freq_cols = col_ids.astype(jnp.float32) / LC
    radius = freq_rows * freq_rows + freq_cols * freq_cols
    defocus = BASE_DEFOCUS + DEFOCUS_STEP * bins[0].astype(jnp.float32)
    phases = math.pi * WAVELENGTH * defocus * radius
    values = -(
        math.sqrt(1.0 - AMPLITUDE * AMPLITUDE) * jnp.sin(phases) + AMPLITUDE * jnp.cos(phases)
    )
    ctf[...] = values * jnp.where(row_ids == 0, 0.5, 1.0)
    for copy in copies:
        copy.wait()
    spectrum[...] = spectrum_of(template, rows, cols)
    half_way = dot(rows[:, :MR], strip[...]).astype(jnp.bfloat16)
    own_part[...] = dot(half_way, cols[...])


def blocks(values):
    upper, lower, edge = values[:PAIRS], values[PAIRS:LR], values[LR:ROWS]
    return tuple(
        block.astype(jnp.float32)
        for part in (upper, lower, edge)
        for block in (part[:, :HALF], part[:, HALF:])
    )


def multiply_back(micro, spectrum, rows_back, product, back):
    for row in range(0, PAIRS, EDGE):
        up, down = slice(row, row + EDGE), slice(PAIRS + row, PAIRS + row + EDGE)
        for col in range(0, HALF, 128):
            real, imag = slice(col, col + 128), slice(HALF + col, HALF + col + 128)
            t_a, t_b, t_d, t_e = (
                spectrum[place].astype(jnp.float32)
                for place in ((up, real), (up, imag), (down, real), (down, imag))
            )
            up_real, up_imag = micro[up, real], micro[up, imag]
            down_real, down_imag = micro[down, real], micro[down, imag]
            s_real, s_imag = t_a - t_e, t_b + t_d
            r_real, r_imag = t_a + t_e, t_b - t_d
            p_real = up_real * s_real - up_imag * s_imag
            p_imag = up_real * s_imag + up_imag * s_real
            q_real = down_real * r_real - down_imag * r_imag
            q_imag = down_real * r_imag + down_imag * r_real
            product[up, real] = (p_real + q_real).astype(jnp.bfloat16)
            product[up, imag] = (p_imag + q_imag).astype(jnp.bfloat16)
            product[down, real] = (q_imag - p_imag).astype(jnp.bfloat16)
            product[down, imag] = (p_real - q_real).astype(jnp.bfloat16)
    t_x = spectrum[LR:ROWS, :HALF].astype(jnp.float32)
    t_y = spectrum[LR:ROWS, HALF:].astype(jnp.float32)
    edge_real, edge_imag = micro[LR:, :HALF], micro[LR:, HALF:]
    product[LR:, :HALF] = (edge_real * t_x - edge_imag * t_y).astype(jnp.bfloat16)
    product[LR:, HALF:] = (edge_real * t_y + edge_imag * t_x).astype(jnp.bfloat16)
    back[...] = dot(rows_back[...], product[...]).astype(jnp.bfloat16)


def far_kernel(far, far_turn, rows, cols, far_packed):
    far_packed[:ROWS, :] = spectrum_of(far, rows, cols)
    far_packed[ROWS:, :HALF] = far_turn[...]
    far_packed[ROWS:, HALF:] = far_turn[...]


def strip_spectrum(halo, own_part, ctf, rows, cols, micro):
    halo_half = dot(rows[:, :MR], halo[...])
    lanes = lax.broadcasted_iota(jnp.int32, halo_half.shape, 1)
    halo_half = jnp.where(lanes < TC - 1, halo_half, 0.0).astype(jnp.bfloat16)
    lanes = lax.broadcasted_iota(jnp.int32, (1, 2 * HALF), 1)
    signs = jnp.where(lanes % 2 == 0, 1.0, -1.0)
    m_a, m_b, m_d, m_e, m_x, m_y = blocks(own_part[...] + signs * dot(halo_half, cols[...]))
    ctf_rows, ctf_edge = ctf[:PAIRS, :], ctf[PAIRS:, :]
    micro[:PAIRS, :HALF] = ctf_rows * (m_a - m_e)
    micro[:PAIRS, HALF:] = -(ctf_rows * (m_b + m_d))
    micro[PAIRS:LR, :HALF] = ctf_rows * (m_a + m_e)
    micro[PAIRS:LR, HALF:] = ctf_rows * (m_d - m_b)
    micro[LR:, :HALF] = ctf_edge * m_x
    micro[LR:, HALF:] = -(ctf_edge * m_y)


def waits_long(choice):
    return pl.when((lax.axis_index("mic") % 4 == 3) == choice)


def early_strip_kernel(
    halo, own_part, ctf, rows, cols, own_spectrum, rows_back, micro, back, product
):
    @waits_long(True)
    def _():
        strip_spectrum(halo, own_part, ctf, rows, cols, micro)
        multiply_back(micro, own_spectrum, rows_back, product, back)


def strip_kernel(
    halo,
    own_part,
    ctf,
    rows,
    cols,
    own_spectrum,
    rows_back,
    far_packed,
    early_micro,
    early_back,
    micro,
    back_own,
    back_far,
    product,
):
    @waits_long(False)
    def _():
        strip_spectrum(halo, own_part, ctf, rows, cols, micro)
        multiply_back(micro, own_spectrum, rows_back, product, back_own)

    @waits_long(True)
    def _():
        micro[...] = early_micro[...]
        back_own[...] = early_back[...]
        multiply_back(early_micro, far_packed, rows_back, product, back_far)


def third_kernel(
    near, micro, far_packed, rows, cols, rows_back, early_far, near_spectrum, back, product
):
    @waits_long(False)
    def _():
        near_spectrum[...] = spectrum_of(near, rows, cols)
        multiply_back(micro, far_packed, rows_back, product, back)

    @waits_long(True)
    def _():
        near_spectrum[...] = spectrum_of(near, rows, cols)
        back[...] = early_far[...]


def last_kernel(
    micro,
    back_own,
    back_far,
    near_spectrum,
    late_packed,
    own_turn,
    near_turn,
    far_packed,
    rows_back,
    cols_back,
    peak,
    total,
    squares,
    orient_cos,
    orient_sin,
    products,
    back_all,
):
    back_all[:MH, :] = back_own[...]
    back_all[MH : 2 * MH, :] = back_far[...]
    multiply_back(micro, near_spectrum, rows_back, products.at[0], back_all.at[2 * MH : 3 * MH])
    multiply_back(micro, late_packed, rows_back, products.at[1], back_all.at[3 * MH :])
    scale = 1.0 / (TS * LR * LC)
    corr_all = dot(back_all[...], cols_back[...]) * scale
    corrs = [corr_all[step * MH : (step + 1) * MH, :] for step in range(STEPS)]
    turns = (own_turn[...], far_packed[ROWS:, :HALF], near_turn[...], late_packed[ROWS:, :HALF])
    sums = None
    for corr, turn in zip(corrs, turns):
        doubled = 2.0 * corr
        weight = jnp.maximum(doubled, 0.0) + jnp.log1p(jnp.exp(-jnp.abs(doubled)))
        cosine, sine = turn[0:1].astype(jnp.float32), turn[8:9].astype(jnp.float32)
        fresh = (corr, corr, corr * corr, weight, weight * cosine, weight * sine)
        if sums is None:
            sums = fresh
        else:
            sums = (jnp.maximum(sums[0], fresh[0]),) + tuple(
                old + new for old, new in zip(sums[1:], fresh[1:])
            )
    peak[...] = sums[0]
    total[...] = sums[1]
    squares[...] = sums[2]
    orient_cos[...] = sums[4] / sums[3]
    orient_sin[...] = sums[5] / sums[3]


def along(array, sources):
    return lax.ppermute(array, "mic", [(source, place) for place, source in enumerate(sources)])


def call(kernel, name, flops, out_shape, in_specs, scratch_shapes=()):
    return pl.pallas_call(
        kernel,
        out_shape=out_shape,
        in_specs=in_specs,
        out_specs=jax.tree.map(lambda _: VMEM, out_shape),
        scratch_shapes=scratch_shapes,
        compiler_params=pltpu.CompilerParams(vmem_limit_bytes=24 * 1024 * 1024),
        cost_estimate=pl.CostEstimate(flops=flops, bytes_accessed=10**3, transcendentals=0),
        name=name,
    )


def body(micrograph, templates, orient_ids, defocus_bins):
    rows_far = jnp.asarray(paired_rows())
    cols_far = jnp.asarray(forward_columns())
    rows_back = jnp.asarray(np.ascontiguousarray(paired_rows()[:, :MH].T))
    cols_back = jnp.asarray(inverse_columns())
    count = lax.axis_size("mic")
    tiles = lax.axis_size("tile")
    strip = micrograph[0]
    own = templates[0]
    near_places = [(d + (1 if d % 2 == 0 else 3)) % count for d in range(count)]
    far_places = [(d + 2) % count for d in range(count)]

    halo = lax.ppermute(strip, "tile", [(i + 1, i) for i in range(tiles - 1)])
    far = along(own, far_places)
    own_turn = call(
        turn_kernel, "turn", COST[0], jax.ShapeDtypeStruct((EDGE, HALF), jnp.bfloat16), [SMEM]
    )(orient_ids)
    near_turn, far_turn = along(own_turn, near_places), along(own_turn, far_places)

    bf16, f32 = jnp.bfloat16, jnp.float32
    spectrum_type = jax.ShapeDtypeStruct((ROWS, 2 * HALF), bf16)
    own_inputs = [
        pltpu.with_memory_space_constraint(x, pltpu.HBM) for x in (strip, own, rows_far, cols_far)
    ]
    rows, cols, template, own_part, ctf, own_spectrum = call(
        first_kernel,
        "own_spectra",
        COST[1],
        (
            jax.ShapeDtypeStruct(rows_far.shape, bf16),
            jax.ShapeDtypeStruct(cols_far.shape, bf16),
            jax.ShapeDtypeStruct(own.shape, bf16),
            jax.ShapeDtypeStruct((ROWS, 2 * HALF), f32),
            jax.ShapeDtypeStruct((PAIRS + EDGE, HALF), f32),
            spectrum_type,
        ),
        [SMEM] + [HBM] * 4,
        [pltpu.VMEM((MR, TC), bf16), pltpu.SemaphoreType.DMA((4,))],
    )(defocus_bins, *own_inputs)
    near = along(own, near_places)
    far, own_spectrum = lax.optimization_barrier((far, own_spectrum))
    back_type = jax.ShapeDtypeStruct((MH, 2 * HALF), bf16)
    strip_types = (jax.ShapeDtypeStruct((ROWS, 2 * HALF), f32), back_type)
    far_packed = call(
        far_kernel,
        "far_spectrum",
        COST[2],
        jax.ShapeDtypeStruct((ROWS + EDGE, 2 * HALF), bf16),
        [VMEM] * 4,
    )(far, far_turn, rows, cols)
    strip_inputs = (halo, own_part, ctf, rows, cols, own_spectrum, rows_back)
    product_scratch = [pltpu.VMEM((ROWS, 2 * HALF), bf16)]
    early_micro, early_back = call(
        early_strip_kernel, "early_strip", COST[3], strip_types, [VMEM] * 7, product_scratch
    )(*strip_inputs)
    far_packed, early_micro = lax.optimization_barrier((far_packed, early_micro))
    late_packed = along(far_packed, [d ^ 1 for d in range(count)])
    micro, back_own, early_far = call(
        strip_kernel, "strip", COST[3], (*strip_types, back_type), [VMEM] * 10, product_scratch
    )(*strip_inputs, far_packed, early_micro, early_back)
    near_spectrum, back_far = call(
        third_kernel,
        "near_and_far",
        COST[4],
        (spectrum_type, back_type),
        [VMEM] * 7,
        product_scratch,
    )(near, micro, far_packed, rows, cols, rows_back, early_far)
    results = call(
        last_kernel,
        "match",
        COST[5],
        (jax.ShapeDtypeStruct((MH, TC), f32),) * 5,
        [VMEM] * 10,
        [pltpu.VMEM((2, ROWS, 2 * HALF), bf16), pltpu.VMEM((STEPS * MH, 2 * HALF), bf16)],
    )(
        micro,
        back_own,
        back_far,
        near_spectrum,
        late_packed,
        own_turn,
        near_turn,
        far_packed,
        rows_back,
        cols_back,
    )
    return tuple(result[None] for result in results)


def solution(mesh):
    tiled = P("mic", None, "tile")
    return jax.shard_map(
        body,
        mesh=mesh,
        in_specs=(tiled, P("mic", None, None), P("mic"), P("mic")),
        out_specs=(tiled,) * 5,
        check_vma=False,
    )
```

```python
import math

import jax
import jax.numpy as jnp
import ml_dtypes
import numpy as np
from jax import lax
from jax.experimental import pallas as pl
from jax.experimental.pallas import tpu as pltpu
from jax.sharding import PartitionSpec as P

TS = 384
TC = 384
MH = 64
STEPS = 4
NANG = 360
MR = 447
LR = 448
LC = 768
HALF = 384
PAIRS = LR // 2
EDGE = 16
ROWS = LR + EDGE

AMPLITUDE = 0.07
WAVELENGTH = 0.0197
BASE_DEFOCUS = 8000.0
DEFOCUS_STEP = 1000.0

COST = (10**5, 10**5, 10**5, 10**5, 10**10, 10**5)

HBM = pl.BlockSpec(memory_space=pltpu.HBM)
SMEM = pl.BlockSpec(memory_space=pltpu.SMEM)
VMEM = pl.BlockSpec(memory_space=pltpu.VMEM)


def trig_pair(left_count, right_count, length):
    ids = np.arange(left_count)[:, None] * np.arange(right_count)[None, :] % length
    angles = ids.astype(np.float32) * np.float32(2.0 * math.pi / length)
    return np.cos(angles), np.sin(angles)


def paired_rows():
    cosine, sine = trig_pair(PAIRS + 1, LR, LR)
    zeros = np.zeros((EDGE - 1, LR), np.float32)
    rows = np.concatenate([cosine[:PAIRS], sine[:PAIRS], cosine[PAIRS:], zeros], axis=0)
    return rows.astype(ml_dtypes.bfloat16)


def forward_columns():
    cosine, sine = trig_pair(TC, HALF, LC)
    return np.concatenate([cosine, sine], axis=1).astype(ml_dtypes.bfloat16)


def inverse_columns():
    cosine, sine = trig_pair(HALF, TC, LC)
    weights = np.where(np.arange(HALF) == 0, 1.0, 2.0).astype(np.float32)[:, None]
    cosine = cosine.astype(ml_dtypes.bfloat16).astype(np.float32) * weights
    sine = sine.astype(ml_dtypes.bfloat16).astype(np.float32) * weights
    return np.concatenate([cosine, -sine], axis=0).astype(ml_dtypes.bfloat16)


def dot(left, right):
    return jnp.dot(left, right, preferred_element_type=jnp.float32)


def store_spectrum(target, template, rows, cols):
    half_way = dot(rows[:, :TS], template[...]).astype(jnp.bfloat16)
    t_a, t_b, t_d, t_e, t_x, t_y = blocks(dot(half_way, cols[...]))
    target[:PAIRS, :HALF] = (t_a - t_e).astype(jnp.bfloat16)
    target[:PAIRS, HALF:] = (t_b + t_d).astype(jnp.bfloat16)
    target[PAIRS:LR, :HALF] = (t_a + t_e).astype(jnp.bfloat16)
    target[PAIRS:LR, HALF:] = (t_b - t_d).astype(jnp.bfloat16)
    target[LR:ROWS, :HALF] = t_x.astype(jnp.bfloat16)
    target[LR:ROWS, HALF:] = t_y.astype(jnp.bfloat16)


def turn_kernel(orient_id, turn):
    turns = jnp.full((EDGE // 2, HALF), orient_id[0]).astype(jnp.float32) * (2.0 * math.pi / NANG)
    turn[...] = jnp.concatenate([jnp.cos(turns), jnp.sin(turns)], axis=0).astype(jnp.bfloat16)


def first_kernel(
    bins,
    strip_far,
    template_far,
    rows_far,
    cols_far,
    rows_back_far,
    cols_back_far,
    rows,
    cols,
    rows_back,
    cols_back,
    template,
    own_part,
    ctf,
    spectrum,
    strip,
    arrived,
):
    pairs = (
        (rows_far, rows),
        (cols_far, cols),
        (template_far, template),
        (strip_far, strip),
        (rows_back_far, rows_back),
        (cols_back_far, cols_back),
    )
    copies = [
        pltpu.make_async_copy(source, target, arrived.at[i])
        for i, (source, target) in enumerate(pairs)
    ]
    for copy in copies:
        copy.start()
    shape = ctf.shape
    row_ids = lax.broadcasted_iota(jnp.int32, shape, 0)
    col_ids = lax.broadcasted_iota(jnp.int32, shape, 1)
    freq_rows = row_ids.astype(jnp.float32) / LR
    freq_cols = col_ids.astype(jnp.float32) / LC
    radius = freq_rows * freq_rows + freq_cols * freq_cols
    defocus = BASE_DEFOCUS + DEFOCUS_STEP * bins[0].astype(jnp.float32)
    phases = math.pi * WAVELENGTH * defocus * radius
    values = -(
        math.sqrt(1.0 - AMPLITUDE * AMPLITUDE) * jnp.sin(phases) + AMPLITUDE * jnp.cos(phases)
    )
    ctf[...] = values * jnp.where(row_ids == 0, 0.5, 1.0)
    for copy in copies:
        copy.wait()
    store_spectrum(spectrum, template, rows, cols)
    half_way = dot(rows[:, :MR], strip[...]).astype(jnp.bfloat16)
    own_part[...] = dot(half_way, cols[...])


def blocks(values):
    upper, lower, edge = values[:PAIRS], values[PAIRS:LR], values[LR:ROWS]
    return tuple(
        block.astype(jnp.float32)
        for part in (upper, lower, edge)
        for block in (part[:, :HALF], part[:, HALF:])
    )


def multiply_back(micro, spectrum, rows_back, product, back):
    for row in range(0, PAIRS, EDGE):
        up, down = slice(row, row + EDGE), slice(PAIRS + row, PAIRS + row + EDGE)
        for col in range(0, HALF, 128):
            real, imag = slice(col, col + 128), slice(HALF + col, HALF + col + 128)
            s_real, s_imag, r_real, r_imag = (
                spectrum[place].astype(jnp.float32)
                for place in ((up, real), (up, imag), (down, real), (down, imag))
            )
            up_real, up_imag = micro[up, real], micro[up, imag]
            down_real, down_imag = micro[down, real], micro[down, imag]
            p_real = up_real * s_real - up_imag * s_imag
            p_imag = up_real * s_imag + up_imag * s_real
            q_real = down_real * r_real - down_imag * r_imag
            q_imag = down_real * r_imag + down_imag * r_real
            product[up, real] = (p_real + q_real).astype(jnp.bfloat16)
            product[up, imag] = (p_imag + q_imag).astype(jnp.bfloat16)
            product[down, real] = (q_imag - p_imag).astype(jnp.bfloat16)
            product[down, imag] = (p_real - q_real).astype(jnp.bfloat16)
    t_x = spectrum[LR:ROWS, :HALF].astype(jnp.float32)
    t_y = spectrum[LR:ROWS, HALF:].astype(jnp.float32)
    edge_real, edge_imag = micro[LR:, :HALF], micro[LR:, HALF:]
    product[LR:, :HALF] = (edge_real * t_x - edge_imag * t_y).astype(jnp.bfloat16)
    product[LR:, HALF:] = (edge_real * t_y + edge_imag * t_x).astype(jnp.bfloat16)
    back[...] = dot(rows_back[...], product[...]).astype(jnp.bfloat16)


def far_kernel(far, far_turn, rows, cols, far_packed):
    store_spectrum(far_packed, far, rows, cols)
    far_packed[ROWS:, :HALF] = far_turn[...]
    far_packed[ROWS:, HALF:] = far_turn[...]


def strip_spectrum(halo, own_part, ctf, rows, cols, micro):
    halo_half = dot(rows[:, :MR], halo[...])
    lanes = lax.broadcasted_iota(jnp.int32, halo_half.shape, 1)
    halo_half = jnp.where(lanes < TC - 1, halo_half, 0.0).astype(jnp.bfloat16)
    lanes = lax.broadcasted_iota(jnp.int32, (1, 2 * HALF), 1)
    signs = jnp.where(lanes % 2 == 0, 1.0, -1.0)
    m_a, m_b, m_d, m_e, m_x, m_y = blocks(own_part[...] + signs * dot(halo_half, cols[...]))
    ctf_rows, ctf_edge = ctf[:PAIRS, :], ctf[PAIRS:, :]
    micro[:PAIRS, :HALF] = ctf_rows * (m_a - m_e)
    micro[:PAIRS, HALF:] = -(ctf_rows * (m_b + m_d))
    micro[PAIRS:LR, :HALF] = ctf_rows * (m_a + m_e)
    micro[PAIRS:LR, HALF:] = ctf_rows * (m_d - m_b)
    micro[LR:, :HALF] = ctf_edge * m_x
    micro[LR:, HALF:] = -(ctf_edge * m_y)


def waits_long(choice):
    return pl.when((lax.axis_index("mic") % 4 == 3) == choice)


def early_strip_kernel(
    halo, own_part, ctf, rows, cols, own_spectrum, rows_back, micro, back, product
):
    @waits_long(True)
    def _():
        strip_spectrum(halo, own_part, ctf, rows, cols, micro)
        multiply_back(micro, own_spectrum, rows_back, product, back)


def strip_kernel(
    halo,
    own_part,
    ctf,
    rows,
    cols,
    own_spectrum,
    rows_back,
    far_packed,
    early_micro,
    early_back,
    micro,
    back_own,
    back_far,
    product,
):
    @waits_long(False)
    def _():
        strip_spectrum(halo, own_part, ctf, rows, cols, micro)
        multiply_back(micro, own_spectrum, rows_back, product, back_own)

    @waits_long(True)
    def _():
        micro[...] = early_micro[...]
        back_own[...] = early_back[...]
        multiply_back(early_micro, far_packed, rows_back, product, back_far)


def third_kernel(
    near, micro, far_packed, rows, cols, rows_back, early_far, near_spectrum, back, product
):
    @waits_long(False)
    def _():
        store_spectrum(near_spectrum, near, rows, cols)
        multiply_back(micro, far_packed, rows_back, product, back)

    @waits_long(True)
    def _():
        store_spectrum(near_spectrum, near, rows, cols)
        back[...] = early_far[...]


def last_kernel(
    micro,
    back_own,
    back_far,
    near_spectrum,
    late_packed,
    own_turn,
    near_turn,
    far_packed,
    rows_back,
    cols_back,
    peak,
    total,
    squares,
    orient_cos,
    orient_sin,
    products,
    back_all,
):
    back_all[:MH, :] = back_own[...]
    back_all[MH : 2 * MH, :] = back_far[...]
    multiply_back(micro, near_spectrum, rows_back, products.at[0], back_all.at[2 * MH : 3 * MH])
    multiply_back(micro, late_packed, rows_back, products.at[1], back_all.at[3 * MH :])
    scale = 1.0 / (TS * LR * LC)
    corr_all = dot(back_all[...], cols_back[...]) * scale
    corrs = [corr_all[step * MH : (step + 1) * MH, :] for step in range(STEPS)]
    turns = (own_turn[...], far_packed[ROWS:, :HALF], near_turn[...], late_packed[ROWS:, :HALF])
    sums = None
    for corr, turn in zip(corrs, turns):
        doubled = 2.0 * corr
        weight = jnp.maximum(doubled, 0.0) + jnp.log1p(jnp.exp(-jnp.abs(doubled)))
        cosine, sine = turn[0:1].astype(jnp.float32), turn[8:9].astype(jnp.float32)
        fresh = (corr, corr, corr * corr, weight, weight * cosine, weight * sine)
        if sums is None:
            sums = fresh
        else:
            sums = (jnp.maximum(sums[0], fresh[0]),) + tuple(
                old + new for old, new in zip(sums[1:], fresh[1:])
            )
    peak[...] = sums[0]
    total[...] = sums[1]
    squares[...] = sums[2]
    orient_cos[...] = sums[4] / sums[3]
    orient_sin[...] = sums[5] / sums[3]


def along(array, sources):
    return lax.ppermute(array, "mic", [(source, place) for place, source in enumerate(sources)])


def call(kernel, name, flops, out_shape, in_specs, scratch_shapes=()):
    return pl.pallas_call(
        kernel,
        out_shape=out_shape,
        in_specs=in_specs,
        out_specs=jax.tree.map(lambda _: VMEM, out_shape),
        scratch_shapes=scratch_shapes,
        compiler_params=pltpu.CompilerParams(vmem_limit_bytes=24 * 1024 * 1024),
        cost_estimate=pl.CostEstimate(flops=flops, bytes_accessed=10**3, transcendentals=0),
        name=name,
    )


def body(micrograph, templates, orient_ids, defocus_bins):
    rows_far = jnp.asarray(paired_rows())
    cols_far = jnp.asarray(forward_columns())
    rows_back_far = jnp.asarray(np.ascontiguousarray(paired_rows()[:, :MH].T))
    cols_back_far = jnp.asarray(inverse_columns())
    count = lax.axis_size("mic")
    tiles = lax.axis_size("tile")
    strip = micrograph[0]
    own = templates[0]
    near_places = [(d + (1 if d % 2 == 0 else 3)) % count for d in range(count)]
    far_places = [(d + 2) % count for d in range(count)]

    halo = lax.ppermute(strip, "tile", [(i + 1, i) for i in range(tiles - 1)])
    far = along(own, far_places)
    own_turn = call(
        turn_kernel, "turn", COST[0], jax.ShapeDtypeStruct((EDGE, HALF), jnp.bfloat16), [SMEM]
    )(orient_ids)
    near_turn, far_turn = along(own_turn, near_places), along(own_turn, far_places)

    bf16, f32 = jnp.bfloat16, jnp.float32
    spectrum_type = jax.ShapeDtypeStruct((ROWS, 2 * HALF), bf16)
    own_inputs = [
        pltpu.with_memory_space_constraint(x, pltpu.HBM) for x in (strip, own, rows_far, cols_far, rows_back_far, cols_back_far)
    ]
    rows, cols, rows_back, cols_back, template, own_part, ctf, own_spectrum = call(
        first_kernel,
        "own_spectra",
        COST[1],
        (
            jax.ShapeDtypeStruct(rows_far.shape, bf16),
            jax.ShapeDtypeStruct(cols_far.shape, bf16),
            jax.ShapeDtypeStruct(rows_back_far.shape, bf16),
            jax.ShapeDtypeStruct(cols_back_far.shape, bf16),
            jax.ShapeDtypeStruct(own.shape, bf16),
            jax.ShapeDtypeStruct((ROWS, 2 * HALF), f32),
            jax.ShapeDtypeStruct((PAIRS + EDGE, HALF), f32),
            spectrum_type,
        ),
        [SMEM] + [HBM] * 6,
        [pltpu.VMEM((MR, TC), bf16), pltpu.SemaphoreType.DMA((6,))],
    )(defocus_bins, *own_inputs)
    near = along(own, near_places)
    far, own_spectrum = lax.optimization_barrier((far, own_spectrum))
    back_type = jax.ShapeDtypeStruct((MH, 2 * HALF), bf16)
    strip_types = (jax.ShapeDtypeStruct((ROWS, 2 * HALF), f32), back_type)
    far_packed = call(
        far_kernel,
        "far_spectrum",
        COST[2],
        jax.ShapeDtypeStruct((ROWS + EDGE, 2 * HALF), bf16),
        [VMEM] * 4,
    )(far, far_turn, rows, cols)
    strip_inputs = (halo, own_part, ctf, rows, cols, own_spectrum, rows_back)
    product_scratch = [pltpu.VMEM((ROWS, 2 * HALF), bf16)]
    early_micro, early_back = call(
        early_strip_kernel, "early_strip", COST[3], strip_types, [VMEM] * 7, product_scratch
    )(*strip_inputs)
    far_packed, early_micro = lax.optimization_barrier((far_packed, early_micro))
    late_packed = along(far_packed, [d ^ 1 for d in range(count)])
    micro, back_own, early_far = call(
        strip_kernel, "strip", COST[3], (*strip_types, back_type), [VMEM] * 10, product_scratch
    )(*strip_inputs, far_packed, early_micro, early_back)
    near_spectrum, back_far = call(
        third_kernel,
        "near_and_far",
        COST[4],
        (spectrum_type, back_type),
        [VMEM] * 7,
        product_scratch,
    )(near, micro, far_packed, rows, cols, rows_back, early_far)
    results = call(
        last_kernel,
        "match",
        COST[5],
        (jax.ShapeDtypeStruct((MH, TC), f32),) * 5,
        [VMEM] * 10,
        [pltpu.VMEM((2, ROWS, 2 * HALF), bf16), pltpu.VMEM((STEPS * MH, 2 * HALF), bf16)],
    )(
        micro,
        back_own,
        back_far,
        near_spectrum,
        late_packed,
        own_turn,
        near_turn,
        far_packed,
        rows_back,
        cols_back,
    )
    return tuple(result[None] for result in results)


def solution(mesh):
    tiled = P("mic", None, "tile")
    return jax.shard_map(
        body,
        mesh=mesh,
        in_specs=(tiled, P("mic", None, None), P("mic"), P("mic")),
        out_specs=(tiled,) * 5,
        check_vma=False,
    )
```

```python
import math

import jax
import jax.numpy as jnp
import ml_dtypes
import numpy as np
from jax import lax
from jax.experimental import pallas as pl
from jax.experimental.pallas import tpu as pltpu
from jax.sharding import PartitionSpec as P

TS = 384
TC = 384
MH = 64
STEPS = 4
NANG = 360
MR = 447
LR = 448
LC = 768
HALF = 384
PAIRS = LR // 2
EDGE = 16
ROWS = LR + EDGE

AMPLITUDE = 0.07
WAVELENGTH = 0.0197
BASE_DEFOCUS = 8000.0
DEFOCUS_STEP = 1000.0

COST = (10**5, 10**5, 10**5, 10**5, 10**10, 10**5)

HBM = pl.BlockSpec(memory_space=pltpu.HBM)
SMEM = pl.BlockSpec(memory_space=pltpu.SMEM)
VMEM = pl.BlockSpec(memory_space=pltpu.VMEM)


def trig_pair(left_count, right_count, length):
    ids = np.arange(left_count)[:, None] * np.arange(right_count)[None, :] % length
    angles = ids.astype(np.float32) * np.float32(2.0 * math.pi / length)
    return np.cos(angles), np.sin(angles)


def paired_rows():
    cosine, sine = trig_pair(PAIRS + 1, LR, LR)
    zeros = np.zeros((EDGE - 1, LR), np.float32)
    rows = np.concatenate([cosine[:PAIRS], sine[:PAIRS], cosine[PAIRS:], zeros], axis=0)
    return rows.astype(ml_dtypes.bfloat16)


def forward_columns():
    cosine, sine = trig_pair(TC, HALF, LC)
    return np.concatenate([cosine, sine], axis=1).astype(ml_dtypes.bfloat16)


def inverse_columns():
    cosine, sine = trig_pair(HALF, TC, LC)
    weights = np.where(np.arange(HALF) == 0, 1.0, 2.0).astype(np.float32)[:, None]
    cosine = cosine.astype(ml_dtypes.bfloat16).astype(np.float32) * weights
    sine = sine.astype(ml_dtypes.bfloat16).astype(np.float32) * weights
    return np.concatenate([cosine, -sine], axis=0).astype(ml_dtypes.bfloat16)


def dot(left, right):
    return jnp.dot(left, right, preferred_element_type=jnp.float32)


def store_spectrum(target, template, rows, cols):
    half_way = dot(rows[:, :TS], template[...]).astype(jnp.bfloat16)
    t_a, t_b, t_d, t_e, t_x, t_y = blocks(dot(half_way, cols[...]))
    target[:PAIRS, :HALF] = (t_a - t_e).astype(jnp.bfloat16)
    target[:PAIRS, HALF:] = (t_b + t_d).astype(jnp.bfloat16)
    target[PAIRS:LR, :HALF] = (t_a + t_e).astype(jnp.bfloat16)
    target[PAIRS:LR, HALF:] = (t_b - t_d).astype(jnp.bfloat16)
    target[LR:ROWS, :HALF] = t_x.astype(jnp.bfloat16)
    target[LR:ROWS, HALF:] = t_y.astype(jnp.bfloat16)


def turn_kernel(orient_id, turn):
    turns = jnp.full((EDGE // 2, HALF), orient_id[0]).astype(jnp.float32) * (2.0 * math.pi / NANG)
    turn[...] = jnp.concatenate([jnp.cos(turns), jnp.sin(turns)], axis=0).astype(jnp.bfloat16)


def first_kernel(
    bins,
    strip_far,
    template_far,
    rows_far,
    cols_far,
    rows_back_far,
    cols_back_far,
    rows,
    cols,
    rows_back,
    cols_back,
    template,
    own_part,
    ctf,
    spectrum,
    strip,
    arrived,
):
    pairs = (
        (rows_far, rows),
        (cols_far, cols),
        (template_far, template),
        (strip_far, strip),
        (rows_back_far, rows_back),
        (cols_back_far, cols_back),
    )
    copies = [
        pltpu.make_async_copy(source, target, arrived.at[i])
        for i, (source, target) in enumerate(pairs)
    ]
    for copy in copies:
        copy.start()
    shape = ctf.shape
    row_ids = lax.broadcasted_iota(jnp.int32, shape, 0)
    col_ids = lax.broadcasted_iota(jnp.int32, shape, 1)
    freq_rows = row_ids.astype(jnp.float32) / LR
    freq_cols = col_ids.astype(jnp.float32) / LC
    radius = freq_rows * freq_rows + freq_cols * freq_cols
    defocus = BASE_DEFOCUS + DEFOCUS_STEP * bins[0].astype(jnp.float32)
    phases = math.pi * WAVELENGTH * defocus * radius
    values = -(
        math.sqrt(1.0 - AMPLITUDE * AMPLITUDE) * jnp.sin(phases) + AMPLITUDE * jnp.cos(phases)
    )
    ctf[...] = values * jnp.where(row_ids == 0, 0.5, 1.0)
    for copy in copies:
        copy.wait()
    store_spectrum(spectrum, template, rows, cols)
    half_way = dot(rows[:, :MR], strip[...]).astype(jnp.bfloat16)
    own_part[...] = dot(half_way, cols[...])


def blocks(values):
    upper, lower, edge = values[:PAIRS], values[PAIRS:LR], values[LR:ROWS]
    return tuple(
        block.astype(jnp.float32)
        for part in (upper, lower, edge)
        for block in (part[:, :HALF], part[:, HALF:])
    )


def multiply_back(micro, spectrum, rows_back, product, back):
    for row in range(0, PAIRS, EDGE):
        up, down = slice(row, row + EDGE), slice(PAIRS + row, PAIRS + row + EDGE)
        for col in range(0, HALF, 128):
            real, imag = slice(col, col + 128), slice(HALF + col, HALF + col + 128)
            s_real, s_imag, r_real, r_imag = (
                spectrum[place].astype(jnp.float32)
                for place in ((up, real), (up, imag), (down, real), (down, imag))
            )
            up_real, up_imag = micro[up, real], micro[up, imag]
            down_real, down_imag = micro[down, real], micro[down, imag]
            p_real = up_real * s_real - up_imag * s_imag
            p_imag = up_real * s_imag + up_imag * s_real
            q_real = down_real * r_real - down_imag * r_imag
            q_imag = down_real * r_imag + down_imag * r_real
            product[up, real] = (p_real + q_real).astype(jnp.bfloat16)
            product[up, imag] = (p_imag + q_imag).astype(jnp.bfloat16)
            product[down, real] = (q_imag - p_imag).astype(jnp.bfloat16)
            product[down, imag] = (p_real - q_real).astype(jnp.bfloat16)
    t_x = spectrum[LR:ROWS, :HALF].astype(jnp.float32)
    t_y = spectrum[LR:ROWS, HALF:].astype(jnp.float32)
    edge_real, edge_imag = micro[LR:, :HALF], micro[LR:, HALF:]
    product[LR:, :HALF] = (edge_real * t_x - edge_imag * t_y).astype(jnp.bfloat16)
    product[LR:, HALF:] = (edge_real * t_y + edge_imag * t_x).astype(jnp.bfloat16)
    back[...] = dot(rows_back[...], product[...]).astype(jnp.bfloat16)


def far_kernel(far, far_turn, rows, cols, far_packed):
    store_spectrum(far_packed, far, rows, cols)
    far_packed[ROWS:, :HALF] = far_turn[...]
    far_packed[ROWS:, HALF:] = far_turn[...]


def strip_spectrum(halo, own_part, ctf, rows, cols, micro):
    halo_half = dot(rows[:, :MR], halo[...])
    lanes = lax.broadcasted_iota(jnp.int32, halo_half.shape, 1)
    halo_half = jnp.where(lanes < TC - 1, halo_half, 0.0).astype(jnp.bfloat16)
    lanes = lax.broadcasted_iota(jnp.int32, (1, 2 * HALF), 1)
    signs = jnp.where(lanes % 2 == 0, 1.0, -1.0)
    m_a, m_b, m_d, m_e, m_x, m_y = blocks(own_part[...] + signs * dot(halo_half, cols[...]))
    ctf_rows, ctf_edge = ctf[:PAIRS, :], ctf[PAIRS:, :]
    micro[:PAIRS, :HALF] = ctf_rows * (m_a - m_e)
    micro[:PAIRS, HALF:] = -(ctf_rows * (m_b + m_d))
    micro[PAIRS:LR, :HALF] = ctf_rows * (m_a + m_e)
    micro[PAIRS:LR, HALF:] = ctf_rows * (m_d - m_b)
    micro[LR:, :HALF] = ctf_edge * m_x
    micro[LR:, HALF:] = -(ctf_edge * m_y)


def waits_long(choice):
    return pl.when((lax.axis_index("mic") % 4 == 3) == choice)


def early_strip_kernel(
    halo, own_part, ctf, rows, cols, own_spectrum, rows_back, micro, back, product
):
    @waits_long(True)
    def _():
        strip_spectrum(halo, own_part, ctf, rows, cols, micro)
        multiply_back(micro, own_spectrum, rows_back, product, back)


def strip_kernel(
    halo,
    own_part,
    ctf,
    rows,
    cols,
    own_spectrum,
    rows_back,
    far_packed,
    early_micro,
    early_back,
    cols_back,
    micro,
    back_own,
    early_corr,
    product,
    backs,
):
    @waits_long(False)
    def _():
        strip_spectrum(halo, own_part, ctf, rows, cols, micro)
        multiply_back(micro, own_spectrum, rows_back, product, back_own)

    @waits_long(True)
    def _():
        micro[...] = early_micro[...]
        back_own[...] = early_back[...]
        backs[:MH, :] = early_back[...]
        multiply_back(early_micro, far_packed, rows_back, product, backs.at[MH:])
        early_corr[...] = dot(backs[...], cols_back[...])


def third_kernel(
    near,
    micro,
    far_packed,
    rows,
    cols,
    rows_back,
    back_own,
    cols_back,
    early_corr,
    near_spectrum,
    corr,
    product,
    backs,
):
    @waits_long(False)
    def _():
        store_spectrum(near_spectrum, near, rows, cols)
        backs[:MH, :] = back_own[...]
        multiply_back(micro, far_packed, rows_back, product, backs.at[MH:])
        corr[...] = dot(backs[...], cols_back[...])

    @waits_long(True)
    def _():
        store_spectrum(near_spectrum, near, rows, cols)
        corr[...] = early_corr[...]


def last_kernel(
    micro,
    corr_early,
    near_spectrum,
    late_packed,
    own_turn,
    near_turn,
    far_packed,
    rows_back,
    cols_back,
    peak,
    total,
    squares,
    orient_cos,
    orient_sin,
    products,
    back_all,
):
    multiply_back(micro, near_spectrum, rows_back, products.at[0], back_all.at[:MH])
    multiply_back(micro, late_packed, rows_back, products.at[1], back_all.at[MH:])
    scale = 1.0 / (TS * LR * LC)
    halves = (corr_early[...] * scale, dot(back_all[...], cols_back[...]) * scale)
    corrs = [half[step * MH : (step + 1) * MH, :] for half in halves for step in range(2)]
    turns = (own_turn[...], far_packed[ROWS:, :HALF], near_turn[...], late_packed[ROWS:, :HALF])
    sums = None
    for corr, turn in zip(corrs, turns):
        doubled = 2.0 * corr
        weight = jnp.maximum(doubled, 0.0) + jnp.log1p(jnp.exp(-jnp.abs(doubled)))
        cosine, sine = turn[0:1].astype(jnp.float32), turn[8:9].astype(jnp.float32)
        fresh = (corr, corr, corr * corr, weight, weight * cosine, weight * sine)
        if sums is None:
            sums = fresh
        else:
            sums = (jnp.maximum(sums[0], fresh[0]),) + tuple(
                old + new for old, new in zip(sums[1:], fresh[1:])
            )
    peak[...] = sums[0]
    total[...] = sums[1]
    squares[...] = sums[2]
    orient_cos[...] = sums[4] / sums[3]
    orient_sin[...] = sums[5] / sums[3]


def along(array, sources):
    return lax.ppermute(array, "mic", [(source, place) for place, source in enumerate(sources)])


def call(kernel, name, flops, out_shape, in_specs, scratch_shapes=()):
    return pl.pallas_call(
        kernel,
        out_shape=out_shape,
        in_specs=in_specs,
        out_specs=jax.tree.map(lambda _: VMEM, out_shape),
        scratch_shapes=scratch_shapes,
        compiler_params=pltpu.CompilerParams(vmem_limit_bytes=24 * 1024 * 1024),
        cost_estimate=pl.CostEstimate(flops=flops, bytes_accessed=10**3, transcendentals=0),
        name=name,
    )


def body(micrograph, templates, orient_ids, defocus_bins):
    rows_far = jnp.asarray(paired_rows())
    cols_far = jnp.asarray(forward_columns())
    rows_back_far = jnp.asarray(np.ascontiguousarray(paired_rows()[:, :MH].T))
    cols_back_far = jnp.asarray(inverse_columns())
    count = lax.axis_size("mic")
    tiles = lax.axis_size("tile")
    strip = micrograph[0]
    own = templates[0]
    near_places = [(d + (1 if d % 2 == 0 else 3)) % count for d in range(count)]
    far_places = [(d + 2) % count for d in range(count)]

    halo = lax.ppermute(strip, "tile", [(i + 1, i) for i in range(tiles - 1)])
    far = along(own, far_places)
    own_turn = call(
        turn_kernel, "turn", COST[0], jax.ShapeDtypeStruct((EDGE, HALF), jnp.bfloat16), [SMEM]
    )(orient_ids)
    near_turn, far_turn = along(own_turn, near_places), along(own_turn, far_places)

    bf16, f32 = jnp.bfloat16, jnp.float32
    spectrum_type = jax.ShapeDtypeStruct((ROWS, 2 * HALF), bf16)
    own_inputs = [
        pltpu.with_memory_space_constraint(x, pltpu.HBM) for x in (strip, own, rows_far, cols_far, rows_back_far, cols_back_far)
    ]
    rows, cols, rows_back, cols_back, template, own_part, ctf, own_spectrum = call(
        first_kernel,
        "own_spectra",
        COST[1],
        (
            jax.ShapeDtypeStruct(rows_far.shape, bf16),
            jax.ShapeDtypeStruct(cols_far.shape, bf16),
            jax.ShapeDtypeStruct(rows_back_far.shape, bf16),
            jax.ShapeDtypeStruct(cols_back_far.shape, bf16),
            jax.ShapeDtypeStruct(own.shape, bf16),
            jax.ShapeDtypeStruct((ROWS, 2 * HALF), f32),
            jax.ShapeDtypeStruct((PAIRS + EDGE, HALF), f32),
            spectrum_type,
        ),
        [SMEM] + [HBM] * 6,
        [pltpu.VMEM((MR, TC), bf16), pltpu.SemaphoreType.DMA((6,))],
    )(defocus_bins, *own_inputs)
    near = along(own, near_places)
    far, own_spectrum = lax.optimization_barrier((far, own_spectrum))
    back_type = jax.ShapeDtypeStruct((MH, 2 * HALF), bf16)
    strip_types = (jax.ShapeDtypeStruct((ROWS, 2 * HALF), f32), back_type)
    far_packed = call(
        far_kernel,
        "far_spectrum",
        COST[2],
        jax.ShapeDtypeStruct((ROWS + EDGE, 2 * HALF), bf16),
        [VMEM] * 4,
    )(far, far_turn, rows, cols)
    strip_inputs = (halo, own_part, ctf, rows, cols, own_spectrum, rows_back)
    product_scratch = [pltpu.VMEM((ROWS, 2 * HALF), bf16)]
    early_micro, early_back = call(
        early_strip_kernel, "early_strip", COST[3], strip_types, [VMEM] * 7, product_scratch
    )(*strip_inputs)
    far_packed, early_micro = lax.optimization_barrier((far_packed, early_micro))
    late_packed = along(far_packed, [d ^ 1 for d in range(count)])
    corr_type = jax.ShapeDtypeStruct((2 * MH, TC), f32)
    corr_scratch = [*product_scratch, pltpu.VMEM((2 * MH, 2 * HALF), bf16)]
    micro, back_own, early_corr = call(
        strip_kernel, "strip", COST[3], (*strip_types, corr_type), [VMEM] * 11, corr_scratch
    )(*strip_inputs, far_packed, early_micro, early_back, cols_back)
    near_spectrum, corr_early = call(
        third_kernel,
        "near_and_far",
        COST[4],
        (spectrum_type, corr_type),
        [VMEM] * 9,
        corr_scratch,
    )(near, micro, far_packed, rows, cols, rows_back, back_own, cols_back, early_corr)
    results = call(
        last_kernel,
        "match",
        COST[5],
        (jax.ShapeDtypeStruct((MH, TC), f32),) * 5,
        [VMEM] * 9,
        [pltpu.VMEM((2, ROWS, 2 * HALF), bf16), pltpu.VMEM((2 * MH, 2 * HALF), bf16)],
    )(
        micro,
        corr_early,
        near_spectrum,
        late_packed,
        own_turn,
        near_turn,
        far_packed,
        rows_back,
        cols_back,
    )
    return tuple(result[None] for result in results)


def solution(mesh):
    tiled = P("mic", None, "tile")
    return jax.shard_map(
        body,
        mesh=mesh,
        in_specs=(tiled, P("mic", None, None), P("mic"), P("mic")),
        out_specs=(tiled,) * 5,
        check_vma=False,
    )
```

```python
import math

import jax
import jax.numpy as jnp
import ml_dtypes
import numpy as np
from jax import lax
from jax.experimental import pallas as pl
from jax.experimental.pallas import tpu as pltpu
from jax.sharding import PartitionSpec as P

TS = 384
TC = 384
MH = 64
STEPS = 4
NANG = 360
MR = 447
LR = 448
LC = 768
HALF = 384
PAIRS = LR // 2
EDGE = 16
ROWS = LR + EDGE

AMPLITUDE = 0.07
WAVELENGTH = 0.0197
BASE_DEFOCUS = 8000.0
DEFOCUS_STEP = 1000.0

COST = (10**5, 10**5, 10**5, 10**5, 10**10, 10**5)

HBM = pl.BlockSpec(memory_space=pltpu.HBM)
SMEM = pl.BlockSpec(memory_space=pltpu.SMEM)
VMEM = pl.BlockSpec(memory_space=pltpu.VMEM)


def trig_pair(left_count, right_count, length):
    ids = np.arange(left_count)[:, None] * np.arange(right_count)[None, :] % length
    angles = ids.astype(np.float32) * np.float32(2.0 * math.pi / length)
    return np.cos(angles), np.sin(angles)


def paired_rows():
    cosine, sine = trig_pair(PAIRS + 1, LR, LR)
    zeros = np.zeros((EDGE - 1, LR), np.float32)
    rows = np.concatenate([cosine[:PAIRS], sine[:PAIRS], cosine[PAIRS:], zeros], axis=0)
    return rows.astype(ml_dtypes.bfloat16)


def forward_columns():
    cosine, sine = trig_pair(TC, HALF, LC)
    return np.concatenate([cosine, sine], axis=1).astype(ml_dtypes.bfloat16)


def inverse_columns():
    cosine, sine = trig_pair(HALF, TC, LC)
    weights = np.where(np.arange(HALF) == 0, 1.0, 2.0).astype(np.float32)[:, None]
    cosine = cosine.astype(ml_dtypes.bfloat16).astype(np.float32) * weights
    sine = sine.astype(ml_dtypes.bfloat16).astype(np.float32) * weights
    return np.concatenate([cosine, -sine], axis=0).astype(ml_dtypes.bfloat16)


def dot(left, right):
    return jnp.dot(left, right, preferred_element_type=jnp.float32)


def store_spectrum(target, template, rows, cols):
    finish_spectrum(target, half_spectrum(template, rows), cols)


def half_spectrum(template, rows):
    return dot(rows[:, :TS], template[...]).astype(jnp.bfloat16)


def finish_spectrum(target, half_way, cols):
    t_a, t_b, t_d, t_e, t_x, t_y = blocks(dot(half_way, cols[...]))
    target[:PAIRS, :HALF] = (t_a - t_e).astype(jnp.bfloat16)
    target[:PAIRS, HALF:] = (t_b + t_d).astype(jnp.bfloat16)
    target[PAIRS:LR, :HALF] = (t_a + t_e).astype(jnp.bfloat16)
    target[PAIRS:LR, HALF:] = (t_b - t_d).astype(jnp.bfloat16)
    target[LR:ROWS, :HALF] = t_x.astype(jnp.bfloat16)
    target[LR:ROWS, HALF:] = t_y.astype(jnp.bfloat16)


def turn_kernel(orient_id, turn):
    turns = jnp.full((EDGE // 2, HALF), orient_id[0]).astype(jnp.float32) * (2.0 * math.pi / NANG)
    turn[...] = jnp.concatenate([jnp.cos(turns), jnp.sin(turns)], axis=0).astype(jnp.bfloat16)


def first_kernel(
    bins,
    strip_far,
    template_far,
    rows_far,
    cols_far,
    rows_back_far,
    cols_back_far,
    rows,
    cols,
    rows_back,
    cols_back,
    template,
    own_part,
    ctf,
    spectrum,
    strip,
    arrived,
):
    pairs = (
        (rows_far, rows),
        (cols_far, cols),
        (template_far, template),
        (strip_far, strip),
        (rows_back_far, rows_back),
        (cols_back_far, cols_back),
    )
    copies = [
        pltpu.make_async_copy(source, target, arrived.at[i])
        for i, (source, target) in enumerate(pairs)
    ]
    for copy in copies:
        copy.start()
    shape = ctf.shape
    row_ids = lax.broadcasted_iota(jnp.int32, shape, 0)
    col_ids = lax.broadcasted_iota(jnp.int32, shape, 1)
    freq_rows = row_ids.astype(jnp.float32) / LR
    freq_cols = col_ids.astype(jnp.float32) / LC
    radius = freq_rows * freq_rows + freq_cols * freq_cols
    defocus = BASE_DEFOCUS + DEFOCUS_STEP * bins[0].astype(jnp.float32)
    phases = math.pi * WAVELENGTH * defocus * radius
    values = -(
        math.sqrt(1.0 - AMPLITUDE * AMPLITUDE) * jnp.sin(phases) + AMPLITUDE * jnp.cos(phases)
    )
    ctf[...] = values * jnp.where(row_ids == 0, 0.5, 1.0)
    for copy in copies[:3]:
        copy.wait()
    store_spectrum(spectrum, template, rows, cols)
    for copy in copies[3:]:
        copy.wait()
    half_way = dot(rows[:, :MR], strip[...]).astype(jnp.bfloat16)
    own_part[...] = dot(half_way, cols[...])


def blocks(values):
    upper, lower, edge = values[:PAIRS], values[PAIRS:LR], values[LR:ROWS]
    return tuple(
        block.astype(jnp.float32)
        for part in (upper, lower, edge)
        for block in (part[:, :HALF], part[:, HALF:])
    )


def multiply_back(micro, spectrum, rows_back, product, back):
    for row in range(0, PAIRS, EDGE):
        up, down = slice(row, row + EDGE), slice(PAIRS + row, PAIRS + row + EDGE)
        for col in range(0, HALF, 128):
            real, imag = slice(col, col + 128), slice(HALF + col, HALF + col + 128)
            s_real, s_imag, r_real, r_imag = (
                spectrum[place].astype(jnp.float32)
                for place in ((up, real), (up, imag), (down, real), (down, imag))
            )
            up_real, up_imag = micro[up, real], micro[up, imag]
            down_real, down_imag = micro[down, real], micro[down, imag]
            p_real = up_real * s_real - up_imag * s_imag
            p_imag = up_real * s_imag + up_imag * s_real
            q_real = down_real * r_real - down_imag * r_imag
            q_imag = down_real * r_imag + down_imag * r_real
            product[up, real] = (p_real + q_real).astype(jnp.bfloat16)
            product[up, imag] = (p_imag + q_imag).astype(jnp.bfloat16)
            product[down, real] = (q_imag - p_imag).astype(jnp.bfloat16)
            product[down, imag] = (p_real - q_real).astype(jnp.bfloat16)
    t_x = spectrum[LR:ROWS, :HALF].astype(jnp.float32)
    t_y = spectrum[LR:ROWS, HALF:].astype(jnp.float32)
    edge_real, edge_imag = micro[LR:, :HALF], micro[LR:, HALF:]
    product[LR:, :HALF] = (edge_real * t_x - edge_imag * t_y).astype(jnp.bfloat16)
    product[LR:, HALF:] = (edge_real * t_y + edge_imag * t_x).astype(jnp.bfloat16)
    back[...] = dot(rows_back[...], product[...]).astype(jnp.bfloat16)


def far_kernel(far, far_turn, rows, cols, far_packed):
    store_spectrum(far_packed, far, rows, cols)
    far_packed[ROWS:, :HALF] = far_turn[...]
    far_packed[ROWS:, HALF:] = far_turn[...]


def strip_spectrum(halo, own_part, ctf, rows, cols, micro):
    halo_half = dot(rows[:, :MR], halo[...])
    lanes = lax.broadcasted_iota(jnp.int32, halo_half.shape, 1)
    halo_half = jnp.where(lanes < TC - 1, halo_half, 0.0).astype(jnp.bfloat16)
    lanes = lax.broadcasted_iota(jnp.int32, (1, 2 * HALF), 1)
    signs = jnp.where(lanes % 2 == 0, 1.0, -1.0)
    m_a, m_b, m_d, m_e, m_x, m_y = blocks(own_part[...] + signs * dot(halo_half, cols[...]))
    ctf_rows, ctf_edge = ctf[:PAIRS, :], ctf[PAIRS:, :]
    micro[:PAIRS, :HALF] = ctf_rows * (m_a - m_e)
    micro[:PAIRS, HALF:] = -(ctf_rows * (m_b + m_d))
    micro[PAIRS:LR, :HALF] = ctf_rows * (m_a + m_e)
    micro[PAIRS:LR, HALF:] = ctf_rows * (m_d - m_b)
    micro[LR:, :HALF] = ctf_edge * m_x
    micro[LR:, HALF:] = -(ctf_edge * m_y)


def waits_long(choice):
    return pl.when((lax.axis_index("mic") % 4 == 3) == choice)


def early_strip_kernel(
    halo, own_part, ctf, rows, cols, own_spectrum, rows_back, micro, back, product
):
    @waits_long(True)
    def _():
        strip_spectrum(halo, own_part, ctf, rows, cols, micro)
        multiply_back(micro, own_spectrum, rows_back, product, back)


def strip_kernel(
    halo,
    own_part,
    ctf,
    rows,
    cols,
    own_spectrum,
    rows_back,
    far_packed,
    early_micro,
    early_back,
    micro,
    back_own,
    back_far,
    product,
):
    @waits_long(False)
    def _():
        strip_spectrum(halo, own_part, ctf, rows, cols, micro)
        multiply_back(micro, own_spectrum, rows_back, product, back_own)

    @waits_long(True)
    def _():
        micro[...] = early_micro[...]
        back_own[...] = early_back[...]
        multiply_back(early_micro, far_packed, rows_back, product, back_far)


def third_kernel(
    near, micro, far_packed, rows, cols, rows_back, early_far, near_spectrum, back, product
):
    @waits_long(False)
    def _():
        near_half = half_spectrum(near, rows)
        multiply_back(micro, far_packed, rows_back, product, back)
        finish_spectrum(near_spectrum, near_half, cols)

    @waits_long(True)
    def _():
        store_spectrum(near_spectrum, near, rows, cols)
        back[...] = early_far[...]


def last_kernel(
    micro,
    back_own,
    back_far,
    near_spectrum,
    late_packed,
    own_turn,
    near_turn,
    far_packed,
    rows_back,
    cols_back,
    peak,
    total,
    squares,
    orient_cos,
    orient_sin,
    products,
    back_all,
):
    back_all[:MH, :] = back_own[...]
    back_all[MH : 2 * MH, :] = back_far[...]
    multiply_back(micro, near_spectrum, rows_back, products.at[0], back_all.at[2 * MH : 3 * MH])
    multiply_back(micro, late_packed, rows_back, products.at[1], back_all.at[3 * MH :])
    scale = 1.0 / (TS * LR * LC)
    corr_all = dot(back_all[...], cols_back[...]) * scale
    corrs = [corr_all[step * MH : (step + 1) * MH, :] for step in range(STEPS)]
    turns = (own_turn[...], far_packed[ROWS:, :HALF], near_turn[...], late_packed[ROWS:, :HALF])
    sums = None
    for corr, turn in zip(corrs, turns):
        doubled = 2.0 * corr
        weight = jnp.maximum(doubled, 0.0) + jnp.log1p(jnp.exp(-jnp.abs(doubled)))
        cosine, sine = turn[0:1].astype(jnp.float32), turn[8:9].astype(jnp.float32)
        fresh = (corr, corr, corr * corr, weight, weight * cosine, weight * sine)
        if sums is None:
            sums = fresh
        else:
            sums = (jnp.maximum(sums[0], fresh[0]),) + tuple(
                old + new for old, new in zip(sums[1:], fresh[1:])
            )
    peak[...] = sums[0]
    total[...] = sums[1]
    squares[...] = sums[2]
    orient_cos[...] = sums[4] / sums[3]
    orient_sin[...] = sums[5] / sums[3]


def along(array, sources):
    return lax.ppermute(array, "mic", [(source, place) for place, source in enumerate(sources)])


def call(kernel, name, flops, out_shape, in_specs, scratch_shapes=()):
    return pl.pallas_call(
        kernel,
        out_shape=out_shape,
        in_specs=in_specs,
        out_specs=jax.tree.map(lambda _: VMEM, out_shape),
        scratch_shapes=scratch_shapes,
        compiler_params=pltpu.CompilerParams(vmem_limit_bytes=24 * 1024 * 1024),
        cost_estimate=pl.CostEstimate(flops=flops, bytes_accessed=10**3, transcendentals=0),
        name=name,
    )


def body(micrograph, templates, orient_ids, defocus_bins):
    rows_far = jnp.asarray(paired_rows())
    cols_far = jnp.asarray(forward_columns())
    rows_back_far = jnp.asarray(np.ascontiguousarray(paired_rows()[:, :MH].T))
    cols_back_far = jnp.asarray(inverse_columns())
    count = lax.axis_size("mic")
    tiles = lax.axis_size("tile")
    strip = micrograph[0]
    own = templates[0]
    near_places = [(d + (1 if d % 2 == 0 else 3)) % count for d in range(count)]
    far_places = [(d + 2) % count for d in range(count)]

    halo = lax.ppermute(strip, "tile", [(i + 1, i) for i in range(tiles - 1)])
    far = along(own, far_places)
    own_turn = call(
        turn_kernel, "turn", COST[0], jax.ShapeDtypeStruct((EDGE, HALF), jnp.bfloat16), [SMEM]
    )(orient_ids)
    near_turn, far_turn = along(own_turn, near_places), along(own_turn, far_places)

    bf16, f32 = jnp.bfloat16, jnp.float32
    spectrum_type = jax.ShapeDtypeStruct((ROWS, 2 * HALF), bf16)
    own_inputs = [
        pltpu.with_memory_space_constraint(x, pltpu.HBM) for x in (strip, own, rows_far, cols_far, rows_back_far, cols_back_far)
    ]
    rows, cols, rows_back, cols_back, template, own_part, ctf, own_spectrum = call(
        first_kernel,
        "own_spectra",
        COST[1],
        (
            jax.ShapeDtypeStruct(rows_far.shape, bf16),
            jax.ShapeDtypeStruct(cols_far.shape, bf16),
            jax.ShapeDtypeStruct(rows_back_far.shape, bf16),
            jax.ShapeDtypeStruct(cols_back_far.shape, bf16),
            jax.ShapeDtypeStruct(own.shape, bf16),
            jax.ShapeDtypeStruct((ROWS, 2 * HALF), f32),
            jax.ShapeDtypeStruct((PAIRS + EDGE, HALF), f32),
            spectrum_type,
        ),
        [SMEM] + [HBM] * 6,
        [pltpu.VMEM((MR, TC), bf16), pltpu.SemaphoreType.DMA((6,))],
    )(defocus_bins, *own_inputs)
    near = along(own, near_places)
    far, own_spectrum = lax.optimization_barrier((far, own_spectrum))
    back_type = jax.ShapeDtypeStruct((MH, 2 * HALF), bf16)
    strip_types = (jax.ShapeDtypeStruct((ROWS, 2 * HALF), f32), back_type)
    far_packed = call(
        far_kernel,
        "far_spectrum",
        COST[2],
        jax.ShapeDtypeStruct((ROWS + EDGE, 2 * HALF), bf16),
        [VMEM] * 4,
    )(far, far_turn, rows, cols)
    strip_inputs = (halo, own_part, ctf, rows, cols, own_spectrum, rows_back)
    product_scratch = [pltpu.VMEM((ROWS, 2 * HALF), bf16)]
    early_micro, early_back = call(
        early_strip_kernel, "early_strip", COST[3], strip_types, [VMEM] * 7, product_scratch
    )(*strip_inputs)
    far_packed, early_micro = lax.optimization_barrier((far_packed, early_micro))
    late_packed = along(far_packed, [d ^ 1 for d in range(count)])
    micro, back_own, early_far = call(
        strip_kernel, "strip", COST[3], (*strip_types, back_type), [VMEM] * 10, product_scratch
    )(*strip_inputs, far_packed, early_micro, early_back)
    near_spectrum, back_far = call(
        third_kernel,
        "near_and_far",
        COST[4],
        (spectrum_type, back_type),
        [VMEM] * 7,
        product_scratch,
    )(near, micro, far_packed, rows, cols, rows_back, early_far)
    results = call(
        last_kernel,
        "match",
        COST[5],
        (jax.ShapeDtypeStruct((MH, TC), f32),) * 5,
        [VMEM] * 10,
        [pltpu.VMEM((2, ROWS, 2 * HALF), bf16), pltpu.VMEM((STEPS * MH, 2 * HALF), bf16)],
    )(
        micro,
        back_own,
        back_far,
        near_spectrum,
        late_packed,
        own_turn,
        near_turn,
        far_packed,
        rows_back,
        cols_back,
    )
    return tuple(result[None] for result in results)


def solution(mesh):
    tiled = P("mic", None, "tile")
    return jax.shard_map(
        body,
        mesh=mesh,
        in_specs=(tiled, P("mic", None, None), P("mic"), P("mic")),
        out_specs=(tiled,) * 5,
        check_vma=False,
    )
```
